32 devices in a mesh: ctx: 8 (over z, y), ch: 4 (over x, core).
Axes of the slice: x: 2, y: 2, z: 4, core: 2. Of those that a mesh axis runs over, the one named last changes fastest.
Arguments:
- conv_input: bfloat16 [32, 128, 8192], P('ctx', None, 'ch'), may hold values from -6 to 6
- gate_signal: bfloat16 [32, 128, 8192], P('ctx', None, 'ch'), may hold values from -6 to 6
- cotangent: bfloat16 [32, 128, 8192], P('ctx', None, 'ch'), may hold values from -6 to 6
- filters: float32 [16, 1024], replicated
- tile_owner: int32 [24], replicated, may hold values from 0 to 7, as said below
- support: int32 [24, 8], replicated, may hold values from -1 to 23, as said below
Outputs:
- gate_grad: bfloat16 [32, 128, 8192], P('ctx', None, 'ch')
- input_grad: bfloat16 [32, 128, 8192], P('ctx', None, 'ch')
- filter_grad: float32 [16, 1024], replicated
The draws below stay inside these ranges and needn't reach their ends.
Inputs may be any that keep to these rules, and one draw needn't show every extreme that they name: tile_owner never falls from one tile to the next; every index of ctx owns from 2 to 4 tiles, some index owns 3 + 1 and some index owns 3 - 1. support[t, k] is t - k where tile t - k belongs to the document of tile t and -1 otherwise; documents are runs of whole tiles, and some document spans 8 tiles or more.
All inputs are finite; a program needn't handle non-finite values.
Results may differ from the reference program's by a relative error of at most 0.0058.
Values may be sent and summed in bfloat16 or wider, within the bound.
A program may use at most 256 MiB of HBM per device.

```python
import math
import jax
import jax.numpy as jnp
from jax import lax

D = 8192
TILE = 128
GROUP = 128
FILTERS = 16
MAXLAG = 8
TILES_DEV = 3
SLOTS = 4
TILES = 24
STORED = 32
LAGS = 1024
N_CTX = 8


def draw_filters(key, part):
    key_noise = jax.random.fold_in(key, 11)
    key_rate = jax.random.fold_in(key, 12)
    lag_axis = jnp.arange(LAGS, dtype=jnp.float32)
    noise_values = jax.random.normal(key_noise, (FILTERS, LAGS), jnp.float32)
    decay_rate = jnp.exp(jax.random.uniform(key_rate, (FILTERS, 1), jnp.float32, jnp.log(1.0 / (8.0 * LAGS)), jnp.log(1.0 / 40.0)))
    return 0.06 * noise_values * jnp.exp(-lag_axis[None, :] * decay_rate)


def draw_tile_owner(key, part):
    device_total = TILES // TILES_DEV
    pair_count = device_total // 2
    pair_moves = jax.random.randint(jax.random.fold_in(key, 21), (pair_count,), -1, 2)
    pair_moves = pair_moves.at[0].set(1)
    paired = jnp.stack([pair_moves, -pair_moves], axis=1).reshape(device_total)
    shuffle = jax.random.permutation(jax.random.fold_in(key, 22), device_total)
    changes = jnp.zeros((device_total,), jnp.int32).at[shuffle].set(paired.astype(jnp.int32))
    run_ends = jnp.cumsum(TILES_DEV + changes)
    tile_ids = jnp.arange(TILES, dtype=jnp.int32)
    return jnp.sum((tile_ids[:, None] >= run_ends[None, :]).astype(jnp.int32), axis=1).astype(jnp.int32)


def draw_support(key, part):
    tile_ids = jnp.arange(TILES, dtype=jnp.int32)
    starts_doc = jax.random.randint(jax.random.fold_in(key, 31), (TILES,), 0, 4) == 0
    long_end = jax.random.randint(jax.random.fold_in(key, 32), (), MAXLAG - 1, TILES)
    held_open = (tile_ids > long_end - MAXLAG + 1) & (tile_ids <= long_end)
    starts_doc = starts_doc & jnp.logical_not(held_open) | (tile_ids == 0)
    doc_begin = lax.cummax(jnp.where(starts_doc, tile_ids, 0), axis=0)
    lag_ids = jnp.arange(MAXLAG, dtype=jnp.int32)
    source = tile_ids[:, None] - lag_ids[None, :]
    return jnp.where(source >= doc_begin[:, None], source, -1).astype(jnp.int32)


def shard_levels(stream_key, extent, split, smallest, high):
    level, own = 1.0, jax.random.fold_in(stream_key, 6)
    for dim, shards_of in split:
        draws = jnp.exp(jax.random.uniform(jax.random.fold_in(own, dim), (shards_of,), jnp.float32, smallest / len(split), high / len(split)))
        level = level * jnp.repeat(draws, extent[dim] // shards_of).reshape([-1 if axis == dim else 1 for axis in range(len(extent))])
    return level


def bell_draw(rng, extent, spread, bound, cuts=(), kind=jnp.bfloat16):
    drawn = jax.random.normal(rng, extent, jnp.float32) * spread
    if len(cuts) > 0:
        drawn = shard_levels(rng, extent, cuts, -0.22, 0.18) * drawn
    return jnp.clip(drawn, min=-bound, max=bound).astype(kind)


def setup_inputs(seed: int = 0) -> dict:
    arg_keys = jax.random.split(jax.random.key(seed), 7)
    return {
        "conv_input": bell_draw(arg_keys[0], (STORED, TILE, D), 1.0, 6.0, ((0, 8), (2, 4))),
        "gate_signal": bell_draw(arg_keys[1], (STORED, TILE, D), 1.0, 6.0, ((0, 8), (2, 4))),
        "cotangent": bell_draw(arg_keys[2], (STORED, TILE, D), 1.0, 6.0, ((0, 8), (2, 4))),
        "filters": draw_filters(jax.random.fold_in(arg_keys[6], 71), 0),
        "tile_owner": draw_tile_owner(jax.random.fold_in(arg_keys[6], 71), 0),
        "support": draw_support(jax.random.fold_in(arg_keys[6], 71), 0),
    }


def filter_blocks(filters, tile_rows, maxlag):
    narrow = filters.astype(jnp.bfloat16)
    row_ids = jnp.arange(tile_rows, dtype=jnp.int32)
    lag_offsets = jnp.arange(maxlag, dtype=jnp.int32)[:, None, None] * tile_rows + row_ids[:, None] - row_ids[None, :]
    picked = jnp.take(narrow, jnp.clip(lag_offsets, 0, filters.shape[1] - 1), axis=1)
    return jnp.where(lag_offsets[None] >= 0, picked, jnp.zeros_like(picked))

def lag_sums(square):
    filter_count, side_length = (square.shape[0], square.shape[1])
    flipped = square[:, :, ::-1]
    padded = jnp.pad(flipped, ((0, 0), (0, 0), (0, side_length)))
    skewed = padded.reshape(filter_count, 2 * side_length * side_length)[:, :side_length * (2 * side_length - 1)]
    return lax.optimization_barrier(jnp.sum(skewed.reshape(filter_count, side_length, 2 * side_length - 1), axis=1))

def spread_lags(squares, lag_count):
    maxlag, filter_count, side_length = (squares.shape[0], squares.shape[1], squares.shape[2])
    accumulated = jnp.zeros((filter_count, (maxlag + 1) * side_length), jnp.float32)
    for lag_index in range(maxlag):
        start_col = lag_index * side_length
        accumulated = accumulated.at[:, start_col:start_col + 2 * side_length - 1].add(lag_sums(squares[lag_index]))
    return accumulated[:, side_length - 1:side_length - 1 + lag_count]

def reference(conv_input, gate_signal, cotangent, filters, tile_owner, support):
    devices = jnp.arange(N_CTX, dtype=jnp.int32)
    counts = lax.optimization_barrier(jnp.sum((tile_owner[None, :] == devices[:, None]).astype(jnp.int32), axis=1))
    starts = (jnp.cumsum(counts) - counts).astype(jnp.int32)
    tile_ids = jnp.arange(TILES, dtype=jnp.int32)
    stored = (tile_owner * SLOTS + tile_ids - starts[tile_owner]).astype(jnp.int32)
    blocks = filter_blocks(filters, TILE, MAXLAG).astype(jnp.float32)
    valid = support >= 0
    source = jnp.clip(support, 0, TILES - 1).astype(jnp.int32)
    column_span = FILTERS * GROUP

    def one_block(block_index):

        def columns_of(values):
            return lax.dynamic_slice_in_dim(values, block_index * column_span, column_span, 2)[stored]
        signal = columns_of(conv_input).astype(jnp.float32).reshape(TILES, TILE, FILTERS, GROUP)
        cot_part = columns_of(cotangent).astype(jnp.float32)
        gate_part = columns_of(gate_signal).astype(jnp.float32)
        weighted = lax.optimization_barrier((gate_part * cot_part).astype(jnp.bfloat16))
        weighted = weighted.astype(jnp.float32).reshape(TILES, TILE, FILTERS, GROUP)
        conv_out = jnp.zeros((TILES, TILE, FILTERS, GROUP), jnp.float32)
        adjoint = jnp.zeros((TILES, TILE, FILTERS, GROUP), jnp.float32)
        squares = []
        for lag_index in range(MAXLAG):
            valid_rows = valid[:, lag_index][:, None, None, None]
            pieces = jnp.where(valid_rows, signal[source[:, lag_index]], 0.0)
            conv_out = conv_out + jnp.einsum('fij,tjfc->tifc', blocks[:, lag_index], pieces)
            squares.append(jnp.einsum('tifc,tjfc->fij', weighted, pieces))
            adjoint_term = jnp.where(valid_rows, jnp.einsum('fji,tjfc->tifc', blocks[:, lag_index], weighted), 0.0)
            adjoint = adjoint.at[source[:, lag_index]].add(adjoint_term)
        gate_part_grad = (cot_part * conv_out.reshape(TILES, TILE, column_span)).astype(jnp.bfloat16)
        input_part_grad = adjoint.reshape(TILES, TILE, column_span).astype(jnp.bfloat16)
        return (gate_part_grad, input_part_grad, jnp.stack(squares))
    results = lax.map(one_block, jnp.arange(D // column_span, dtype=jnp.int32))
    gate_tiles = jnp.transpose(results[0], (1, 2, 0, 3)).reshape(TILES, TILE, D)
    input_tiles = jnp.transpose(results[1], (1, 2, 0, 3)).reshape(TILES, TILE, D)
    gate_grad = jnp.zeros((N_CTX * SLOTS, TILE, D), jnp.bfloat16).at[stored].set(gate_tiles)
    input_grad = jnp.zeros((N_CTX * SLOTS, TILE, D), jnp.bfloat16).at[stored].set(input_tiles)
    norm_factor = 1.0 / math.sqrt(TILES * TILE * D / FILTERS)
    filter_grad = spread_lags(lax.optimization_barrier(jnp.sum(results[2], axis=0)), LAGS) * norm_factor
    return (gate_grad, input_grad, filter_grad)
```

```python
import functools
import math

import jax
import jax.numpy as jnp
from jax import lax
from jax.experimental import pallas as pl
from jax.experimental.pallas import tpu as pltpu
from jax.sharding import PartitionSpec as P

GROUP = 128
LEAD = 8
LO = 4
MESH = pl.DeviceIdType.MESH


def copy_to(src, dst, send, recv, ctx):
    return pltpu.make_async_remote_copy(
        src_ref=src,
        dst_ref=dst,
        send_sem=send,
        recv_sem=recv,
        device_id={"ctx": ctx},
        device_id_type=MESH,
    )


def kernel(
    n_ctx,
    tab,
    x_ref,
    gate_ref,
    cot_ref,
    taps_ref,
    rtaps_ref,
    fmask_ref,
    bmask_ref,
    gg_ref,
    ig_ref,
    fg_ref,
    xr,
    wr,
    ws,
    hx,
    gw,
    sx,
    tw,
    rc,
    ra,
    sc,
    sa,
    cx,
    cw,
    mat_a,
    mat_b,
    rhs,
    vv,
    co,
    ao,
    y_send,
    y_recv,
    z_send,
    z_recv,
):
    slots, rows, channels = x_ref.shape
    half = channels // 2
    chunks = half // GROUP
    lags = taps_ref.shape[1]
    own = 2 * slots
    reach = lags - 1
    f32, bf16 = jnp.float32, jnp.bfloat16
    me = lax.axis_index("ctx")
    pair = me // 2
    side = me % 2
    partner = me + 1 - 2 * side
    up, down = me + 2, me - 2
    has_up = pair < n_ctx // 2 - 1
    has_down = pair > 0
    t_s, t_t, t_w, t_v, t_mine, t_theirs = 0, 7, 14, 29, 44, 48

    barrier = pltpu.get_barrier_semaphore()
    pl.semaphore_signal(barrier, inc=1, device_id={"ctx": partner}, device_id_type=MESH)

    @pl.when(has_up)
    def _():
        pl.semaphore_signal(barrier, inc=1, device_id={"ctx": up}, device_id_type=MESH)

    @pl.when(has_down)
    def _():
        pl.semaphore_signal(barrier, inc=1, device_id={"ctx": down}, device_id_type=MESH)

    pl.semaphore_wait(barrier, 1 + has_up.astype(jnp.int32) + has_down.astype(jnp.int32))

    co[own] = jnp.zeros((rows, GROUP), f32)
    ao[own] = jnp.zeros((rows, GROUP), f32)

    @pl.when(jnp.logical_not(has_down))
    def _():
        hx[...] = jnp.zeros(hx.shape, bf16)

    @pl.when(jnp.logical_not(has_up))
    def _():
        gw[...] = jnp.zeros(gw.shape, bf16)

    def lanes(which, c):
        return pl.ds(pl.multiple_of(which * half + c * GROUP, GROUP), GROUP)

    def x_copy(c):
        return copy_to(
            x_ref.at[:, :, lanes(1 - side, c)], xr.at[c], y_send.at[0, c], y_recv.at[0, c], partner
        )

    def w_copy(c):
        return copy_to(ws.at[c], wr.at[c], y_send.at[1, c], y_recv.at[1, c], partner)

    def c_copy(c):
        return copy_to(sc.at[c], rc.at[c], y_send.at[2, c], y_recv.at[2, c], partner)

    def a_copy(c):
        return copy_to(sa.at[c], ra.at[c], y_send.at[3, c], y_recv.at[3, c], partner)

    def x_up(c, part):
        span = pl.ds(0, LO) if part == 0 else pl.ds(LO, reach - LO)
        return copy_to(
            sx.at[c, span], hx.at[c, span], z_send.at[part, c], z_recv.at[part, c], up
        )

    def w_down(c, part):
        span = pl.ds(0, LO) if part == 0 else pl.ds(LO, reach - LO)
        return copy_to(
            tw.at[c, span], gw.at[c, span], z_send.at[2 + part, c], z_recv.at[2 + part, c], down
        )

    def weigh(j, which, c):
        at = lanes(which, c)
        return (gate_ref[j, :, at].astype(f32) * cot_ref[j, :, at].astype(f32)).astype(bf16)

    def launch(c):
        x_copy(c).start()
        for j in range(slots):
            ws[c, j] = weigh(j, 1 - side, c)
        w_copy(c).start()

    def send_halo(c, part):
        for q in range(LO) if part == 0 else range(LO, reach):
            sx[c, q] = cx[c, tab[t_s + q]]
            tw[c, q] = cw[c, tab[t_t + q]]

        @pl.when(has_up)
        def _():
            x_up(c, part).start()

        @pl.when(has_down)
        def _():
            w_down(c, part).start()

    def take_halo(c, part):
        @pl.when(has_down)
        def _():
            x_up(c, part).wait_recv()

        @pl.when(has_up)
        def _():
            w_down(c, part).wait_recv()

        for q in range(LO) if part == 0 else range(LO, reach):
            cx[c, own + q] = hx[c, q]
            cw[c, own + q] = gw[c, q]

    def gather_pair(c):
        mine, theirs = side * slots, (1 - side) * slots
        for j in range(slots):
            cx[c, mine + j] = x_ref[j, :, lanes(side, c)]
            cw[c, mine + j] = weigh(j, side, c)
        x_copy(c).wait_recv()
        w_copy(c).wait_recv()
        for j in range(slots):
            cx[c, theirs + j] = xr[c, j]
            cw[c, theirs + j] = wr[c, j]
        send_halo(c, 0)

    def relay(c):
        take_halo(c, 0)
        send_halo(c, 1)

    def work(c):
        row = lax.broadcasted_iota(jnp.int32, (rows, GROUP), 0)
        lane = lax.broadcasted_iota(jnp.int32, (rows, GROUP), 1)
        lower, upper = row >= lane, lane >= row
        before_a = jnp.zeros((rows, GROUP), f32)
        before_b = jnp.zeros((rows, GROUP), f32)
        for k in range(lags):
            now_a = pltpu.roll(
                jnp.broadcast_to(rtaps_ref[c, k : k + 1, :], (rows, GROUP)),
                0, 1, stride=1, stride_axis=0,
            )
            now_b = pltpu.roll(
                jnp.broadcast_to(taps_ref[c, k : k + 1, :], (rows, GROUP)),
                0, 1, stride=1, stride_axis=0,
            )
            at = pl.ds((lags - 1 - k) * GROUP, GROUP)
            mat_a[:, at] = jnp.where(lower, now_a, before_a).astype(bf16)
            mat_b[:, pl.ds(k * GROUP, GROUP)] = jnp.where(upper, now_b, before_b).astype(bf16)
            before_a, before_b = now_a, now_b

        take_halo(c, 1)

        def fill(cur, base, mask):
            for r in range(own + reach):
                tile = cur[c, tab[base + r]].reshape(rows // 16, 16, GROUP)
                for u in range(max(0, r - reach), min(own, r + 1)):
                    b = r - u
                    masked = tile * mask[u * lags + b][None]
                    rhs[pl.ds(b * rows, rows), pl.ds(u * GROUP, GROUP)] = masked.reshape(rows, GROUP)

        fill(cw, t_v, bmask_ref)
        out = jnp.dot(mat_b[...], rhs[...], preferred_element_type=f32)
        for u in range(own):
            ao[u] = out[:, u * GROUP : (u + 1) * GROUP]
            vv[:, pl.ds(u * GROUP, GROUP)] = cw[c, tab[t_v + u]]
        for j in range(slots):
            ig_ref[j, :, lanes(side, c)] = ao[tab[t_mine + j]].astype(bf16)
            sa[c, j] = ao[tab[t_theirs + j]].astype(bf16)
        a_copy(c).start()
        fill(cx, t_w, fmask_ref)
        out = jnp.dot(mat_a[...], rhs[...], preferred_element_type=f32)
        for u in range(own):
            co[u] = out[:, u * GROUP : (u + 1) * GROUP]
        for j in range(slots):
            at = lanes(side, c)
            gg_ref[j, :, at] = (cot_ref[j, :, at].astype(f32) * co[tab[t_mine + j]]).astype(bf16)
            sc[c, j] = co[tab[t_theirs + j]].astype(bf16)
        c_copy(c).start()
        flip = (row + lane == rows - 1).astype(f32).astype(bf16)
        turned = jnp.dot(flip, vv[...], preferred_element_type=f32).astype(bf16)
        square = lax.dot_general(
            turned, rhs[...], (((1,), (1,)), ((), ())), preferred_element_type=f32
        )
        for k in range(lags):
            here = square[:, (lags - 1 - k) * rows : (lags - k) * rows]
            if k < lags - 1:
                above = square[:, (lags - 2 - k) * rows : (lags - 1 - k) * rows]
            else:
                above = jnp.zeros_like(here)
            skewed = pltpu.roll(
                jnp.where(row + lane <= rows - 1, here, above), 0, 1, stride=1, stride_axis=0
            )
            fg_ref[c, k : k + 1, :] = jnp.sum(skewed, axis=0, keepdims=True)

    def finish(c):
        a_copy(c).wait_recv()
        c_copy(c).wait_recv()
        at = lanes(1 - side, c)
        for j in range(slots):
            ig_ref[j, :, at] = ra[c, j]
            gg_ref[j, :, at] = (
                cot_ref[j, :, at].astype(f32) * rc[c, j].astype(f32)
            ).astype(bf16)

    for c in range(min(LEAD, chunks)):
        launch(c)

    @pl.loop(0, chunks + 3)
    def _(s):
        if LEAD < chunks:
            @pl.when(s + LEAD < chunks)
            def _():
                launch(s + LEAD)

        @pl.when(s < chunks)
        def _():
            gather_pair(s)

        @pl.when((s >= 1) & (s < chunks + 1))
        def _():
            relay(s - 1)

        @pl.when((s >= 2) & (s < chunks + 2))
        def _():
            work(s - 2)

        @pl.when(s >= 3)
        def _():
            finish(s - 3)

    @pl.loop(0, chunks)
    def _(c):
        x_copy(c).wait_send()
        w_copy(c).wait_send()
        a_copy(c).wait_send()
        c_copy(c).wait_send()

        @pl.when(has_up)
        def _():
            x_up(c, 0).wait_send()
            x_up(c, 1).wait_send()

        @pl.when(has_down)
        def _():
            w_down(c, 0).wait_send()
            w_down(c, 1).wait_send()


def tables(tile_owner, support, n_ctx, slots, me):
    total = tile_owner.shape[0]
    maxlag = support.shape[1]
    own, reach = 2 * slots, maxlag - 1
    pair, side = me // 2, me % 2
    count0 = jnp.sum((tile_owner == 2 * pair).astype(jnp.int32))
    count1 = jnp.sum((tile_owner == 2 * pair + 1).astype(jnp.int32))
    first = jnp.sum((tile_owner < 2 * pair).astype(jnp.int32))
    n = count0 + count1

    def place(u):
        return jnp.clip(jnp.where(u < count0, u, slots + u - count0), 0, own - 1)

    q = jnp.arange(reach, dtype=jnp.int32)
    r = jnp.arange(own + reach, dtype=jnp.int32)
    j = jnp.arange(slots, dtype=jnp.int32)
    last = own + reach - 1
    t_s = jnp.where(q < n, place(n - 1 - q), jnp.clip(own + q - n, 0, last))
    t_t = jnp.where(q < n, place(q), jnp.clip(own + q - n, 0, last))
    t_w = jnp.where(r < reach, own + reach - 1 - r, place(r - reach))
    t_v = jnp.where(r < n, place(r), jnp.clip(own + r - n, 0, last))
    u0 = jnp.where(j < count0, j, own)
    u1 = jnp.where(j < count1, j + count0, own)
    t_mine = jnp.where(side == 0, u0, u1)
    t_theirs = jnp.where(side == 0, u1, u0)
    tab = jnp.concatenate([t_s, t_t, t_w, t_v, t_mine, t_theirs]).astype(jnp.int32)

    u = jnp.arange(own, dtype=jnp.int32)[:, None]
    k = jnp.arange(maxlag, dtype=jnp.int32)[None, :]
    live = u < n
    reader = first + u
    ok_f = live & (support[jnp.clip(reader, 0, total - 1), k] >= 0)
    later = reader + k
    ok_b = live & (later < total) & (support[jnp.clip(later, 0, total - 1), k] >= 0)
    spread = lambda ok: jnp.broadcast_to(
        ok.reshape(-1)[:, None, None], (own * maxlag, 16, GROUP)
    ).astype(jnp.bfloat16)
    return tab, spread(ok_f[:, ::-1]), spread(ok_b)


def per_device(conv_input, gate_signal, cotangent, filters, tile_owner, support):
    slots, rows, channels = conv_input.shape
    lags = support.shape[1]
    filter_count, taps = filters.shape
    n_ctx = lax.axis_size("ctx")
    me = lax.axis_index("ctx")
    half = channels // 2
    chunks = half // GROUP
    own, reach = 2 * slots, lags - 1
    tab, fmask, bmask = tables(tile_owner, support, n_ctx, slots, me)
    turn = lambda a: jnp.roll(a[..., ::-1], 1, axis=-1)
    narrow = filters.astype(jnp.bfloat16).astype(jnp.float32)
    at = (me % 2) * chunks
    mine = lax.dynamic_slice_in_dim(narrow, at, chunks, 0).reshape(chunks, lags, rows)
    bf16, f32 = jnp.bfloat16, jnp.float32
    vmem = pl.BlockSpec(memory_space=pltpu.VMEM)
    whole = jax.ShapeDtypeStruct(conv_input.shape, bf16)
    part = lambda count: pltpu.VMEM((chunks, count, rows, GROUP), bf16)
    gate_grad, input_grad, sums = pl.pallas_call(
        functools.partial(kernel, n_ctx),
        out_shape=(whole, whole, jax.ShapeDtypeStruct((chunks, lags, rows), f32)),
        in_specs=[pl.BlockSpec(memory_space=pltpu.SMEM)] + [vmem] * 7,
        out_specs=(vmem, vmem, vmem),
        scratch_shapes=[
            part(slots),
            part(slots),
            part(slots),
            part(reach),
            part(reach),
            part(reach),
            part(reach),
            part(slots),
            part(slots),
            part(slots),
            part(slots),
            part(own + reach),
            part(own + reach),
            pltpu.VMEM((rows, lags * rows), bf16),
            pltpu.VMEM((rows, lags * rows), bf16),
            pltpu.VMEM((lags * rows, own * GROUP), bf16),
            pltpu.VMEM((rows, own * GROUP), bf16),
            pltpu.VMEM((own + 1, rows, GROUP), f32),
            pltpu.VMEM((own + 1, rows, GROUP), f32),
            pltpu.SemaphoreType.DMA((4, chunks)),
            pltpu.SemaphoreType.DMA((4, chunks)),
            pltpu.SemaphoreType.DMA((4, chunks)),
            pltpu.SemaphoreType.DMA((4, chunks)),
        ],
        compiler_params=pltpu.CompilerParams(
            collective_id=0, has_side_effects=True, vmem_limit_bytes=56 * 2**20
        ),
        cost_estimate=pl.CostEstimate(
            flops=6 * rows * rows * own * lags * half,
            bytes_accessed=10 * slots * rows * channels,
            transcendentals=0,
        ),
    )(tab, conv_input, gate_signal, cotangent, mine, turn(mine), fmask, bmask)
    norm = 1.0 / math.sqrt(
        tile_owner.shape[0] * rows * channels * lax.axis_size("ch") / filter_count
    )
    local = jnp.zeros((filter_count, taps), f32)
    local = lax.dynamic_update_slice_in_dim(
        local, sums[..., ::-1].reshape(chunks, taps), at, 0
    )
    filter_grad = lax.psum(local, ("ctx", "ch")) * norm
    return gate_grad, input_grad, filter_grad


def solution(mesh):
    return jax.shard_map(
        per_device,
        mesh=mesh,
        in_specs=(P("ctx", None, "ch"), P("ctx", None, "ch"), P("ctx", None, "ch"), P(), P(), P()),
        out_specs=(P("ctx", None, "ch"), P("ctx", None, "ch"), P()),
        check_vma=False,
    )
```

```python
import functools
import math

import jax
import jax.numpy as jnp
from jax import lax
from jax.experimental import pallas as pl
from jax.experimental.pallas import tpu as pltpu
from jax.sharding import PartitionSpec as P

GROUP = 128
LEAD = 4
LAG = 5
LATE = 2
LO = 4
MESH = pl.DeviceIdType.MESH


def copy_to(src, dst, send, recv, to, axis="ctx"):
    return pltpu.make_async_remote_copy(
        src_ref=src,
        dst_ref=dst,
        send_sem=send,
        recv_sem=recv,
        device_id={axis: to},
        device_id_type=MESH,
    )


def kernel(
    n_ctx,
    n_ch,
    norm,
    owner_ref,
    support_ref,
    x_ref,
    gate_ref,
    cot_ref,
    taps_ref,
    gg_ref,
    ig_ref,
    fg_ref,
    xr,
    wr,
    ws,
    hx,
    gw,
    sx,
    tw,
    rc,
    ra,
    sc,
    sa,
    cx,
    cw,
    mat_a,
    mat_b,
    rhs,
    vv,
    co,
    ao,
    tab,
    taps,
    fmask_ref,
    bmask_ref,
    sums,
    ch_sums,
    ch_got,
    ctx_got,
    y_send,
    y_recv,
    z_send,
    z_recv,
    ch_send,
    ch_recv,
    ctx_send,
    ctx_recv,
):
    slots, rows, channels = x_ref.shape
    half = channels // 2
    chunks = half // GROUP
    lags = support_ref.shape[1]
    total = owner_ref.shape[0]
    own = 2 * slots
    reach = lags - 1
    f32, bf16 = jnp.float32, jnp.bfloat16
    me = lax.axis_index("ctx")
    pair = me // 2
    side = me % 2
    partner = me + 1 - 2 * side
    up, down = me + 2, me - 2
    has_up = pair < n_ctx // 2 - 1
    has_down = pair > 0
    t_s, t_t, t_w, t_v, t_mine, t_theirs = 0, 7, 14, 29, 44, 48

    my_ch = lax.axis_index("ch")
    batches = [(0, chunks - LATE), (chunks - LATE, LATE)]

    def other(d, axis, mine, size):
        return {axis: lax.rem(mine + d, size)}

    barrier = pltpu.get_barrier_semaphore()

    @pl.loop(1, n_ctx)
    def _(d):
        pl.semaphore_signal(
            barrier, inc=1, device_id=other(d, "ctx", me, n_ctx), device_id_type=MESH
        )

    @pl.loop(1, n_ch)
    def _(d):
        pl.semaphore_signal(
            barrier, inc=1, device_id=other(d, "ch", my_ch, n_ch), device_id_type=MESH
        )

    pl.semaphore_wait(barrier, n_ctx + n_ch - 2)

    co[own] = jnp.zeros((rows, GROUP), f32)
    ao[own] = jnp.zeros((rows, GROUP), f32)

    @pl.when(jnp.logical_not(has_down))
    def _():
        hx[...] = jnp.zeros(hx.shape, bf16)

    @pl.when(jnp.logical_not(has_up))
    def _():
        gw[...] = jnp.zeros(gw.shape, bf16)

    def lanes(which, c):
        return pl.ds(pl.multiple_of(which * half + c * GROUP, GROUP), GROUP)

    def x_copy(c):
        return copy_to(
            x_ref.at[:, :, lanes(1 - side, c)], xr.at[c], y_send.at[0, c], y_recv.at[0, c], partner
        )

    def w_copy(c):
        return copy_to(ws.at[c], wr.at[c], y_send.at[1, c], y_recv.at[1, c], partner)

    def c_copy(c):
        return copy_to(sc.at[c], rc.at[c], y_send.at[2, c], y_recv.at[2, c], partner)

    def a_copy(c):
        return copy_to(sa.at[c], ra.at[c], y_send.at[3, c], y_recv.at[3, c], partner)

    def x_up(c, part):
        span = pl.ds(0, LO) if part == 0 else pl.ds(LO, reach - LO)
        return copy_to(
            sx.at[c, span], hx.at[c, span], z_send.at[part, c], z_recv.at[part, c], up
        )

    def w_down(c, part):
        span = pl.ds(0, LO) if part == 0 else pl.ds(LO, reach - LO)
        return copy_to(
            tw.at[c, span], gw.at[c, span], z_send.at[2 + part, c], z_recv.at[2 + part, c], down
        )

    def weigh(j, which, c):
        at = lanes(which, c)
        return (gate_ref[j, :, at].astype(f32) * cot_ref[j, :, at].astype(f32)).astype(bf16)

    def launch(c):
        x_copy(c).start()
        for j in range(slots):
            ws[c, j] = weigh(j, 1 - side, c)
        w_copy(c).start()

    def send_halo(c, part):
        for q in range(LO) if part == 0 else range(LO, reach):
            sx[c, q] = cx[c, tab[t_s + q]]
            tw[c, q] = cw[c, tab[t_t + q]]

        @pl.when(has_up)
        def _():
            x_up(c, part).start()

        @pl.when(has_down)
        def _():
            w_down(c, part).start()

    def take_halo(c, part):
        @pl.when(has_down)
        def _():
            x_up(c, part).wait_recv()

        @pl.when(has_up)
        def _():
            w_down(c, part).wait_recv()

        for q in range(LO) if part == 0 else range(LO, reach):
            cx[c, own + q] = hx[c, q]
            cw[c, own + q] = gw[c, q]

    def gather_pair(c):
        mine, theirs = side * slots, (1 - side) * slots
        for j in range(slots):
            cx[c, mine + j] = x_ref[j, :, lanes(side, c)]
            cw[c, mine + j] = weigh(j, side, c)
        x_copy(c).wait_recv()
        w_copy(c).wait_recv()
        for j in range(slots):
            cx[c, theirs + j] = xr[c, j]
            cw[c, theirs + j] = wr[c, j]
        send_halo(c, 0)

    def relay(c):
        take_halo(c, 0)
        send_halo(c, 1)

    def work(c):
        row = lax.broadcasted_iota(jnp.int32, (rows, GROUP), 0)
        lane = lax.broadcasted_iota(jnp.int32, (rows, GROUP), 1)
        upper = lane >= row
        before = jnp.zeros((rows, GROUP), f32)
        for k in range(lags):
            now = pltpu.roll(
                jnp.broadcast_to(taps[c, k : k + 1, :], (rows, GROUP)),
                0, 1, stride=1, stride_axis=0,
            )
            block = jnp.where(upper, now, before)
            at = pl.ds((lags - 1 - k) * GROUP, GROUP)
            mat_a[:, at] = block.T.astype(bf16)
            mat_b[:, pl.ds(k * GROUP, GROUP)] = block.astype(bf16)
            before = now

        take_halo(c, 1)

        def fill(cur, base, mask):
            for r in range(own + reach):
                tile = cur[c, tab[base + r]].reshape(rows // 16, 16, GROUP)
                for u in range(max(0, r - reach), min(own, r + 1)):
                    b = r - u
                    masked = tile * mask[u * lags + b][None]
                    rhs[pl.ds(b * rows, rows), pl.ds(u * GROUP, GROUP)] = masked.reshape(rows, GROUP)

        fill(cw, t_v, bmask_ref)
        out = jnp.dot(mat_b[...], rhs[...], preferred_element_type=f32)
        for u in range(own):
            ao[u] = out[:, u * GROUP : (u + 1) * GROUP]
            vv[:, pl.ds(u * GROUP, GROUP)] = cw[c, tab[t_v + u]]
        for j in range(slots):
            ig_ref[j, :, lanes(side, c)] = ao[tab[t_mine + j]].astype(bf16)
            sa[c, j] = ao[tab[t_theirs + j]].astype(bf16)
        a_copy(c).start()
        fill(cx, t_w, fmask_ref)
        out = jnp.dot(mat_a[...], rhs[...], preferred_element_type=f32)
        for u in range(own):
            co[u] = out[:, u * GROUP : (u + 1) * GROUP]
        for j in range(slots):
            at = lanes(side, c)
            gg_ref[j, :, at] = (cot_ref[j, :, at].astype(f32) * co[tab[t_mine + j]]).astype(bf16)
            sc[c, j] = co[tab[t_theirs + j]].astype(bf16)
        c_copy(c).start()
        flip = (row + lane == rows - 1).astype(f32).astype(bf16)
        turned = jnp.dot(flip, vv[...], preferred_element_type=f32).astype(bf16)
        square = lax.dot_general(
            turned, rhs[...], (((1,), (1,)), ((), ())), preferred_element_type=f32
        )
        for k in range(lags):
            here = square[:, (lags - 1 - k) * rows : (lags - k) * rows]
            if k < lags - 1:
                above = square[:, (lags - 2 - k) * rows : (lags - 1 - k) * rows]
            else:
                above = jnp.zeros_like(here)
            skewed = pltpu.roll(
                jnp.where(row + lane <= rows - 1, here, above), 0, 1, stride=1, stride_axis=0
            )
            sums[c, k : k + 1, :] = jnp.sum(skewed, axis=0, keepdims=True)

    def finish(c):
        a_copy(c).wait_recv()
        c_copy(c).wait_recv()
        at = lanes(1 - side, c)
        for j in range(slots):
            ig_ref[j, :, at] = ra[c, j]
            gg_ref[j, :, at] = (
                cot_ref[j, :, at].astype(f32) * rc[c, j].astype(f32)
            ).astype(bf16)

    def over_ch(b, d, sender):
        start, size = batches[b]
        return copy_to(
            sums.at[pl.ds(start, size)],
            ch_got.at[sender, pl.ds(start, size)],
            ch_send.at[b, d],
            ch_recv.at[b, sender],
            lax.rem(my_ch + d, n_ch),
            "ch",
        )

    def over_ctx(b, d, sender):
        start, size = batches[b]
        return copy_to(
            ch_sums.at[pl.ds(start, size)],
            ctx_got.at[sender, pl.ds(start, size)],
            ctx_send.at[b, d],
            ctx_recv.at[b, sender],
            lax.rem(me + d, n_ctx),
        )

    def sum_over_ch(b):
        @pl.loop(1, n_ch)
        def _(d):
            over_ch(b, d, my_ch).start()

        at = pl.ds(*batches[b])
        ch_got[my_ch, at] = sums[at]

    def sum_over_ctx(b):
        @pl.loop(1, n_ch)
        def _(d):
            over_ch(b, d, lax.rem(my_ch + d, n_ch)).wait_recv()

        at = pl.ds(*batches[b])
        acc = ch_got[0, at]
        for i in range(1, n_ch):
            acc = acc + ch_got[i, at]
        ch_sums[at] = acc

        @pl.loop(1, n_ctx)
        def _(d):
            over_ctx(b, d, me).start()

        ctx_got[me, at] = acc

    def end_sums():
        for b in range(2):
            @pl.loop(1, n_ctx)
            def _(d):
                over_ctx(b, d, lax.rem(me + d, n_ctx)).wait_recv()

        row = lax.broadcasted_iota(jnp.int32, (GROUP, GROUP), 0)
        lane = lax.broadcasted_iota(jnp.int32, (GROUP, GROUP), 1)
        flip = (row + lane == GROUP - 1).astype(f32)
        for parity in range(2):
            acc = lax.fori_loop(
                1,
                n_ctx // 2,
                lambda i, acc: acc + ctx_got[2 * i + parity],
                ctx_got[parity],
            )
            flat = jnp.dot(
                acc.reshape(chunks * lags, GROUP),
                flip,
                preferred_element_type=f32,
                precision=lax.Precision.HIGHEST,
            )
            whole = flat.reshape(chunks, lags, GROUP) * norm
            for c in range(chunks):
                for k in range(lags):
                    fg_ref[
                        parity * chunks + c : parity * chunks + c + 1,
                        k * GROUP : (k + 1) * GROUP,
                    ] = whole[c, k : k + 1]

    def make_tables():
        def count(t, found):
            holder = owner_ref[t]
            one = lambda hit: hit.astype(jnp.int32)
            return (
                found[0] + one(holder == 2 * pair),
                found[1] + one(holder == 2 * pair + 1),
                found[2] + one(holder < 2 * pair),
            )

        zero = jnp.int32(0)
        count0, count1, first = lax.fori_loop(0, total, count, (zero, zero, zero))
        n = count0 + count1

        mine = taps_ref[pl.ds(pl.multiple_of(side * chunks, chunks), chunks), :]
        mine = mine.astype(bf16).astype(f32)
        for c in range(chunks):
            for k in range(lags):
                taps[c, k : k + 1, :] = mine[c : c + 1, k * GROUP : (k + 1) * GROUP]

        def place(u):
            return jnp.clip(jnp.where(u < count0, u, slots + u - count0), 0, own - 1)

        def beyond(q):
            return jnp.clip(own + q - n, 0, own + reach - 1)

        for q in range(reach):
            tab[t_s + q] = jnp.where(q < n, place(n - 1 - q), beyond(q))
            tab[t_t + q] = jnp.where(q < n, place(q), beyond(q))
        for r in range(own + reach):
            tab[t_w + r] = own + reach - 1 - r if r < reach else place(r - reach)
            tab[t_v + r] = jnp.where(r < n, place(r), beyond(r))
        for j in range(slots):
            at0 = jnp.where(j < count0, j, own)
            at1 = jnp.where(j < count1, j + count0, own)
            tab[t_mine + j] = jnp.where(side == 0, at0, at1)
            tab[t_theirs + j] = jnp.where(side == 0, at1, at0)

        def put(mask, at, ok):
            value = ok.astype(jnp.int32).astype(f32)
            mask[at] = jnp.full((16, GROUP), value, f32).astype(bf16)

        for u in range(own):
            for k in range(lags):
                live = u < n
                found = support_ref[jnp.clip(first + u, 0, total - 1), k] >= 0
                put(fmask_ref, u * lags + lags - 1 - k, live & found)
                later = first + u + k
                found = support_ref[jnp.clip(later, 0, total - 1), k] >= 0
                put(bmask_ref, u * lags + k, live & found & (later < total))

    for c in range(min(LEAD, chunks)):
        launch(c)
    make_tables()

    @pl.loop(0, chunks + LAG)
    def _(s):
        if LEAD < chunks:
            @pl.when(s + LEAD < chunks)
            def _():
                launch(s + LEAD)

        @pl.when(s < chunks)
        def _():
            gather_pair(s)

        @pl.when((s >= 1) & (s < chunks + 1))
        def _():
            relay(s - 1)

        @pl.when((s >= 2) & (s < chunks + 2))
        def _():
            work(s - 2)

        for b, (start, size) in enumerate(batches):
            @pl.when(s == start + size + 1)
            def _():
                sum_over_ch(b)

            @pl.when(s == start + size + 2)
            def _():
                sum_over_ctx(b)

        @pl.when(s >= LAG)
        def _():
            finish(s - LAG)

    end_sums()
    for b in range(2):
        @pl.loop(1, n_ch)
        def _(d):
            over_ch(b, d, my_ch).wait_send()

        @pl.loop(1, n_ctx)
        def _(d):
            over_ctx(b, d, me).wait_send()

    @pl.loop(0, chunks)
    def _(c):
        x_copy(c).wait_send()
        w_copy(c).wait_send()
        a_copy(c).wait_send()
        c_copy(c).wait_send()

        @pl.when(has_up)
        def _():
            x_up(c, 0).wait_send()
            x_up(c, 1).wait_send()

        @pl.when(has_down)
        def _():
            w_down(c, 0).wait_send()
            w_down(c, 1).wait_send()


def per_device(conv_input, gate_signal, cotangent, filters, tile_owner, support):
    slots, rows, channels = conv_input.shape
    lags = support.shape[1]
    filter_count, taps = filters.shape
    n_ctx = lax.axis_size("ctx")
    n_ch = lax.axis_size("ch")
    half = channels // 2
    chunks = half // GROUP
    own, reach = 2 * slots, lags - 1
    norm = 1.0 / math.sqrt(
        tile_owner.shape[0] * rows * channels * lax.axis_size("ch") / filter_count
    )
    bf16, f32 = jnp.bfloat16, jnp.float32
    vmem = pl.BlockSpec(memory_space=pltpu.VMEM)
    whole = jax.ShapeDtypeStruct(conv_input.shape, bf16)
    part = lambda count: pltpu.VMEM((chunks, count, rows, GROUP), bf16)
    return pl.pallas_call(
        functools.partial(kernel, n_ctx, n_ch, norm),
        out_shape=(whole, whole, jax.ShapeDtypeStruct(filters.shape, f32)),
        in_specs=[pl.BlockSpec(memory_space=pltpu.SMEM)] * 2 + [vmem] * 4,
        out_specs=(vmem, vmem, vmem),
        scratch_shapes=[
            part(slots),
            part(slots),
            part(slots),
            part(reach),
            part(reach),
            part(reach),
            part(reach),
            part(slots),
            part(slots),
            part(slots),
            part(slots),
            part(own + reach),
            part(own + reach),
            pltpu.VMEM((rows, lags * rows), bf16),
            pltpu.VMEM((rows, lags * rows), bf16),
            pltpu.VMEM((lags * rows, own * GROUP), bf16),
            pltpu.VMEM((rows, own * GROUP), bf16),
            pltpu.VMEM((own + 1, rows, GROUP), f32),
            pltpu.VMEM((own + 1, rows, GROUP), f32),
            pltpu.SMEM((52,), jnp.int32),
            pltpu.VMEM((chunks, lags, GROUP), f32),
            pltpu.VMEM((own * lags, 16, GROUP), bf16),
            pltpu.VMEM((own * lags, 16, GROUP), bf16),
            pltpu.VMEM((chunks, lags, GROUP), f32),
            pltpu.VMEM((chunks, lags, GROUP), f32),
            pltpu.VMEM((n_ch, chunks, lags, GROUP), f32),
            pltpu.VMEM((n_ctx, chunks, lags, GROUP), f32),
            pltpu.SemaphoreType.DMA((4, chunks)),
            pltpu.SemaphoreType.DMA((4, chunks)),
            pltpu.SemaphoreType.DMA((4, chunks)),
            pltpu.SemaphoreType.DMA((4, chunks)),
            pltpu.SemaphoreType.DMA((2, n_ch)),
            pltpu.SemaphoreType.DMA((2, n_ch)),
            pltpu.SemaphoreType.DMA((2, n_ctx)),
            pltpu.SemaphoreType.DMA((2, n_ctx)),
        ],
        compiler_params=pltpu.CompilerParams(
            collective_id=0, has_side_effects=True, vmem_limit_bytes=56 * 2**20
        ),
        cost_estimate=pl.CostEstimate(
            flops=6 * rows * rows * own * lags * half,
            bytes_accessed=10 * slots * rows * channels,
            transcendentals=0,
        ),
    )(tile_owner, support, conv_input, gate_signal, cotangent, filters)


def solution(mesh):
    return jax.shard_map(
        per_device,
        mesh=mesh,
        in_specs=(P("ctx", None, "ch"), P("ctx", None, "ch"), P("ctx", None, "ch"), P(), P(), P()),
        out_specs=(P("ctx", None, "ch"), P("ctx", None, "ch"), P()),
        check_vma=False,
    )
```

```python
import functools
import math

import jax
import jax.numpy as jnp
from jax import lax
from jax.experimental import pallas as pl
from jax.experimental.pallas import tpu as pltpu
from jax.sharding import PartitionSpec as P

GROUP = 128
LEAD = 2
LAG = 5
LATE = 2
LO = 4
MESH = pl.DeviceIdType.MESH


def copy_to(src, dst, send, recv, to, axis="ctx"):
    return pltpu.make_async_remote_copy(
        src_ref=src,
        dst_ref=dst,
        send_sem=send,
        recv_sem=recv,
        device_id={axis: to},
        device_id_type=MESH,
    )


def kernel(
    n_ctx,
    n_ch,
    norm,
    owner_ref,
    support_ref,
    x_ref,
    gate_ref,
    cot_ref,
    taps_ref,
    conv_ref,
    ig_ref,
    fg_ref,
    xo,
    gate_own,
    gate_far,
    cot_own,
    cot_far,
    conv_own,
    ig_own,
    xr,
    wr,
    ws,
    hx,
    gw,
    sx,
    tw,
    rc,
    ra,
    sc,
    sa,
    cx,
    cw,
    mat_a,
    mat_b,
    rhs,
    vv,
    co,
    ao,
    tab,
    taps,
    fmask_ref,
    bmask_ref,
    sums,
    ch_sums,
    ch_got,
    ctx_got,
    y_send,
    y_recv,
    z_send,
    z_recv,
    ch_send,
    ch_recv,
    ctx_send,
    ctx_recv,
    in_sem,
    x_sem,
    out_sem,
):
    slots, rows, channels = x_ref.shape
    half = channels // 2
    chunks = half // GROUP
    lags = support_ref.shape[0]
    total = owner_ref.shape[0]
    own = 2 * slots
    reach = lags - 1
    f32, bf16 = jnp.float32, jnp.bfloat16
    me = lax.axis_index("ctx")
    pair = me // 2
    side = me % 2
    partner = me + 1 - 2 * side
    up, down = me + 2, me - 2
    has_up = pair < n_ctx // 2 - 1
    has_down = pair > 0
    t_s, t_t, t_w, t_v, t_mine, t_theirs = 0, 7, 14, 29, 44, 48

    my_ch = lax.axis_index("ch")
    batches = [(0, chunks - LATE), (chunks - LATE, LATE)]

    def other(d, axis, mine, size):
        return {axis: lax.rem(mine + d, size)}

    def lanes(which, c):
        return pl.ds(pl.multiple_of(which * half + c * GROUP, GROUP), GROUP)

    def load(kind, which, c):
        src = (gate_ref, cot_ref)[kind]
        at = 0 if which is side else 1
        dst = ((gate_own, gate_far), (cot_own, cot_far))[kind][at]
        return pltpu.make_async_copy(
            src.at[:, :, lanes(which, c)], dst.at[c], in_sem.at[kind, at, c]
        )

    def load_x(c):
        return pltpu.make_async_copy(x_ref.at[:, :, lanes(side, c)], xo.at[c], x_sem.at[c])

    def store(kind, which, c):
        dst = (conv_ref, ig_ref)[kind].at[:, :, lanes(which, c)]
        if which is side:
            src = (conv_own, ig_own)[kind].at[c]
        else:
            src = (rc, ra)[kind].at[c]
        at = 0 if which is side else 1
        return pltpu.make_async_copy(src, dst, out_sem.at[kind, at, c])

    far = 1 - side

    @pl.loop(0, chunks)
    def _(c):
        load(0, far, c).start()
        load(1, far, c).start()
        load_x(c).start()
        load(0, side, c).start()
        load(1, side, c).start()

    barrier = pltpu.get_barrier_semaphore()

    @pl.loop(1, n_ctx)
    def _(d):
        pl.semaphore_signal(
            barrier, inc=1, device_id=other(d, "ctx", me, n_ctx), device_id_type=MESH
        )

    @pl.loop(1, n_ch)
    def _(d):
        pl.semaphore_signal(
            barrier, inc=1, device_id=other(d, "ch", my_ch, n_ch), device_id_type=MESH
        )

    pl.semaphore_wait(barrier, n_ctx + n_ch - 2)

    co[own] = jnp.zeros((rows, GROUP), f32)
    ao[own] = jnp.zeros((rows, GROUP), f32)

    @pl.when(jnp.logical_not(has_down))
    def _():
        hx[...] = jnp.zeros(hx.shape, bf16)

    @pl.when(jnp.logical_not(has_up))
    def _():
        gw[...] = jnp.zeros(gw.shape, bf16)

    def x_copy(c):
        return copy_to(
            x_ref.at[:, :, lanes(far, c)], xr.at[c], y_send.at[0, c], y_recv.at[0, c], partner
        )

    def w_copy(c):
        return copy_to(ws.at[c], wr.at[c], y_send.at[1, c], y_recv.at[1, c], partner)

    def c_copy(c):
        return copy_to(sc.at[c], rc.at[c], y_send.at[2, c], y_recv.at[2, c], partner)

    def a_copy(c):
        return copy_to(sa.at[c], ra.at[c], y_send.at[3, c], y_recv.at[3, c], partner)

    def x_up(c, part):
        span = pl.ds(0, LO) if part == 0 else pl.ds(LO, reach - LO)
        return copy_to(
            sx.at[c, span], hx.at[c, span], z_send.at[part, c], z_recv.at[part, c], up
        )

    def w_down(c, part):
        span = pl.ds(0, LO) if part == 0 else pl.ds(LO, reach - LO)
        return copy_to(
            tw.at[c, span], gw.at[c, span], z_send.at[2 + part, c], z_recv.at[2 + part, c], down
        )

    def weigh(j, which, c):
        gate, cot = (gate_own, cot_own) if which is side else (gate_far, cot_far)
        return (gate[c, j].astype(f32) * cot[c, j].astype(f32)).astype(bf16)

    def launch(c):
        x_copy(c).start()
        load(0, far, c).wait()
        load(1, far, c).wait()
        for j in range(slots):
            ws[c, j] = weigh(j, far, c)
        w_copy(c).start()

    def send_halo(c, part):
        for q in range(LO) if part == 0 else range(LO, reach):
            sx[c, q] = cx[c, tab[t_s + q]]
            tw[c, q] = cw[c, tab[t_t + q]]

        @pl.when(has_up)
        def _():
            x_up(c, part).start()

        @pl.when(has_down)
        def _():
            w_down(c, part).start()

    def take_halo(c, part):
        @pl.when(has_down)
        def _():
            x_up(c, part).wait_recv()

        @pl.when(has_up)
        def _():
            w_down(c, part).wait_recv()

        for q in range(LO) if part == 0 else range(LO, reach):
            cx[c, own + q] = hx[c, q]
            cw[c, own + q] = gw[c, q]

    def gather_pair(c):
        mine, theirs = side * slots, far * slots
        load_x(c).wait()
        load(0, side, c).wait()
        load(1, side, c).wait()
        for j in range(slots):
            cx[c, mine + j] = xo[c, j]
            cw[c, mine + j] = weigh(j, side, c)
        x_copy(c).wait_recv()
        w_copy(c).wait_recv()
        for j in range(slots):
            cx[c, theirs + j] = xr[c, j]
            cw[c, theirs + j] = wr[c, j]
        send_halo(c, 0)

    def relay(c):
        take_halo(c, 0)
        send_halo(c, 1)

    def work(c):
        row = lax.broadcasted_iota(jnp.int32, (rows, GROUP), 0)
        lane = lax.broadcasted_iota(jnp.int32, (rows, GROUP), 1)
        upper = lane >= row
        before = jnp.zeros((rows, GROUP), f32)
        for k in range(lags):
            now = pltpu.roll(
                jnp.broadcast_to(taps[c, k : k + 1, :], (rows, GROUP)),
                0, 1, stride=1, stride_axis=0,
            )
            block = jnp.where(upper, now, before)
            at = pl.ds((lags - 1 - k) * GROUP, GROUP)
            mat_a[:, at] = block.T.astype(bf16)
            mat_b[:, pl.ds(k * GROUP, GROUP)] = block.astype(bf16)
            before = now

        take_halo(c, 1)

        def fill(cur, base, mask):
            for r in range(own + reach):
                tile = cur[c, tab[base + r]].reshape(rows // 16, 16, GROUP)
                for u in range(max(0, r - reach), min(own, r + 1)):
                    b = r - u
                    masked = tile * mask[u * lags + b][None]
                    rhs[pl.ds(b * rows, rows), pl.ds(u * GROUP, GROUP)] = masked.reshape(rows, GROUP)

        fill(cw, t_v, bmask_ref)
        out = jnp.dot(mat_b[...], rhs[...], preferred_element_type=f32)
        for u in range(own):
            ao[u] = out[:, u * GROUP : (u + 1) * GROUP]
            vv[:, pl.ds(u * GROUP, GROUP)] = cw[c, tab[t_v + u]]
        for j in range(slots):
            sa[c, j] = ao[tab[t_theirs + j]].astype(bf16)
        a_copy(c).start()
        for j in range(slots):
            ig_own[c, j] = ao[tab[t_mine + j]].astype(bf16)
        store(1, side, c).start()
        fill(cx, t_w, fmask_ref)
        out = jnp.dot(mat_a[...], rhs[...], preferred_element_type=f32)
        for u in range(own):
            co[u] = out[:, u * GROUP : (u + 1) * GROUP]
        for j in range(slots):
            sc[c, j] = co[tab[t_theirs + j]].astype(bf16)
        c_copy(c).start()
        for j in range(slots):
            conv_own[c, j] = co[tab[t_mine + j]].astype(bf16)
        store(0, side, c).start()
        flip = (row + lane == rows - 1).astype(f32).astype(bf16)
        turned = jnp.dot(flip, vv[...], preferred_element_type=f32).astype(bf16)
        square = lax.dot_general(
            turned, rhs[...], (((1,), (1,)), ((), ())), preferred_element_type=f32
        )
        for k in range(lags):
            here = square[:, (lags - 1 - k) * rows : (lags - k) * rows]
            if k < lags - 1:
                above = square[:, (lags - 2 - k) * rows : (lags - 1 - k) * rows]
            else:
                above = jnp.zeros_like(here)
            skewed = pltpu.roll(
                jnp.where(row + lane <= rows - 1, here, above), 0, 1, stride=1, stride_axis=0
            )
            sums[c, k : k + 1, :] = jnp.sum(skewed, axis=0, keepdims=True)

    def finish(c):
        a_copy(c).wait_recv()
        store(1, far, c).start()
        c_copy(c).wait_recv()
        store(0, far, c).start()

    def over_ch(b, d, sender):
        start, size = batches[b]
        return copy_to(
            sums.at[pl.ds(start, size)],
            ch_got.at[sender, pl.ds(start, size)],
            ch_send.at[b, d],
            ch_recv.at[b, sender],
            lax.rem(my_ch + d, n_ch),
            "ch",
        )

    def over_ctx(b, d, sender):
        start, size = batches[b]
        return copy_to(
            ch_sums.at[pl.ds(start, size)],
            ctx_got.at[sender, pl.ds(start, size)],
            ctx_send.at[b, d],
            ctx_recv.at[b, sender],
            lax.rem(me + d, n_ctx),
        )

    def sum_over_ch(b):
        @pl.loop(1, n_ch)
        def _(d):
            over_ch(b, d, my_ch).start()

        at = pl.ds(*batches[b])
        ch_got[my_ch, at] = sums[at]

    def sum_over_ctx(b):
        @pl.loop(1, n_ch)
        def _(d):
            over_ch(b, d, lax.rem(my_ch + d, n_ch)).wait_recv()

        at = pl.ds(*batches[b])
        acc = ch_got[0, at]
        for i in range(1, n_ch):
            acc = acc + ch_got[i, at]
        ch_sums[at] = acc

        @pl.loop(1, n_ctx)
        def _(d):
            over_ctx(b, d, me).start()

        ctx_got[me, at] = acc

    def end_sums():
        for b in range(2):
            @pl.loop(1, n_ctx)
            def _(d):
                over_ctx(b, d, lax.rem(me + d, n_ctx)).wait_recv()

        row = lax.broadcasted_iota(jnp.int32, (GROUP, GROUP), 0)
        lane = lax.broadcasted_iota(jnp.int32, (GROUP, GROUP), 1)
        flip = (row + lane == GROUP - 1).astype(f32)
        for parity in range(2):
            acc = lax.fori_loop(
                1,
                n_ctx // 2,
                lambda i, acc: acc + ctx_got[2 * i + parity],
                ctx_got[parity],
            )
            flat = jnp.dot(
                acc.reshape(chunks * lags, GROUP),
                flip,
                preferred_element_type=f32,
                precision=lax.Precision.HIGHEST,
            )
            whole = flat.reshape(chunks, lags, GROUP) * norm
            for c in range(chunks):
                for k in range(lags):
                    fg_ref[
                        parity * chunks + c : parity * chunks + c + 1,
                        k * GROUP : (k + 1) * GROUP,
                    ] = whole[c, k : k + 1]

    def make_tables():
        def count(t, found):
            holder = owner_ref[t]
            one = lambda hit: hit.astype(jnp.int32)
            return (
                found[0] + one(holder == 2 * pair),
                found[1] + one(holder == 2 * pair + 1),
                found[2] + one(holder < 2 * pair),
            )

        zero = jnp.int32(0)
        count0, count1, first = lax.fori_loop(0, total, count, (zero, zero, zero))
        n = count0 + count1

        mine = taps_ref[pl.ds(pl.multiple_of(side * chunks, chunks), chunks), :]
        mine = mine.astype(bf16).astype(f32)
        for c in range(chunks):
            for k in range(lags):
                taps[c, k : k + 1, :] = mine[c : c + 1, k * GROUP : (k + 1) * GROUP]

        def place(u):
            return jnp.clip(jnp.where(u < count0, u, slots + u - count0), 0, own - 1)

        def beyond(q):
            return jnp.clip(own + q - n, 0, own + reach - 1)

        for q in range(reach):
            tab[t_s + q] = jnp.where(q < n, place(n - 1 - q), beyond(q))
            tab[t_t + q] = jnp.where(q < n, place(q), beyond(q))
        for r in range(own + reach):
            tab[t_w + r] = own + reach - 1 - r if r < reach else place(r - reach)
            tab[t_v + r] = jnp.where(r < n, place(r), beyond(r))
        for j in range(slots):
            at0 = jnp.where(j < count0, j, own)
            at1 = jnp.where(j < count1, j + count0, own)
            tab[t_mine + j] = jnp.where(side == 0, at0, at1)
            tab[t_theirs + j] = jnp.where(side == 0, at1, at0)

        def put(mask, at, ok):
            value = ok.astype(jnp.int32).astype(f32)
            mask[at] = jnp.full((16, GROUP), value, f32).astype(bf16)

        for u in range(own):
            for k in range(lags):
                live = u < n
                found = support_ref[k, jnp.clip(first + u, 0, total - 1)] >= 0
                put(fmask_ref, u * lags + lags - 1 - k, live & found)
                later = first + u + k
                found = support_ref[k, jnp.clip(later, 0, total - 1)] >= 0
                put(bmask_ref, u * lags + k, live & found & (later < total))

    for c in range(min(LEAD, chunks)):
        launch(c)
    make_tables()

    @pl.loop(0, chunks + LAG)
    def _(s):
        if LEAD < chunks:
            @pl.when(s + LEAD < chunks)
            def _():
                launch(s + LEAD)

        @pl.when(s < chunks)
        def _():
            gather_pair(s)

        @pl.when((s >= 1) & (s < chunks + 1))
        def _():
            relay(s - 1)

        @pl.when((s >= 2) & (s < chunks + 2))
        def _():
            work(s - 2)

        for b, (start, size) in enumerate(batches):
            @pl.when(s == start + size + 1)
            def _():
                sum_over_ch(b)

            @pl.when(s == start + size + 2)
            def _():
                sum_over_ctx(b)

        @pl.when(s >= LAG)
        def _():
            finish(s - LAG)

    end_sums()
    for b in range(2):
        @pl.loop(1, n_ch)
        def _(d):
            over_ch(b, d, my_ch).wait_send()

        @pl.loop(1, n_ctx)
        def _(d):
            over_ctx(b, d, me).wait_send()

    @pl.loop(0, chunks)
    def _(c):
        for kind in range(2):
            store(kind, side, c).wait()
            store(kind, far, c).wait()
        x_copy(c).wait_send()
        w_copy(c).wait_send()
        a_copy(c).wait_send()
        c_copy(c).wait_send()

        @pl.when(has_up)
        def _():
            x_up(c, 0).wait_send()
            x_up(c, 1).wait_send()

        @pl.when(has_down)
        def _():
            w_down(c, 0).wait_send()
            w_down(c, 1).wait_send()


def per_device(conv_input, gate_signal, cotangent, filters, tile_owner, support):
    slots, rows, channels = conv_input.shape
    lags = support.shape[1]
    filter_count, taps = filters.shape
    n_ctx = lax.axis_size("ctx")
    n_ch = lax.axis_size("ch")
    half = channels // 2
    chunks = half // GROUP
    own, reach = 2 * slots, lags - 1
    norm = 1.0 / math.sqrt(
        tile_owner.shape[0] * rows * channels * lax.axis_size("ch") / filter_count
    )
    bf16, f32 = jnp.bfloat16, jnp.float32
    vmem = pl.BlockSpec(memory_space=pltpu.VMEM)
    whole = jax.ShapeDtypeStruct(conv_input.shape, bf16)
    part = lambda count: pltpu.VMEM((chunks, count, rows, GROUP), bf16)
    hbm = pl.BlockSpec(memory_space=pl.ANY)
    conv, input_grad, filter_grad = pl.pallas_call(
        functools.partial(kernel, n_ctx, n_ch, norm),
        out_shape=(whole, whole, jax.ShapeDtypeStruct(filters.shape, f32)),
        in_specs=[pl.BlockSpec(memory_space=pltpu.SMEM)] * 2 + [hbm] * 3 + [vmem],
        out_specs=(hbm, hbm, vmem),
        scratch_shapes=[
            part(slots),
            part(slots),
            part(slots),
            part(slots),
            part(slots),
            part(slots),
            part(slots),
            part(slots),
            part(slots),
            part(slots),
            part(reach),
            part(reach),
            part(reach),
            part(reach),
            part(slots),
            part(slots),
            part(slots),
            part(slots),
            part(own + reach),
            part(own + reach),
            pltpu.VMEM((rows, lags * rows), bf16),
            pltpu.VMEM((rows, lags * rows), bf16),
            pltpu.VMEM((lags * rows, own * GROUP), bf16),
            pltpu.VMEM((rows, own * GROUP), bf16),
            pltpu.VMEM((own + 1, rows, GROUP), f32),
            pltpu.VMEM((own + 1, rows, GROUP), f32),
            pltpu.SMEM((52,), jnp.int32),
            pltpu.VMEM((chunks, lags, GROUP), f32),
            pltpu.VMEM((own * lags, 16, GROUP), bf16),
            pltpu.VMEM((own * lags, 16, GROUP), bf16),
            pltpu.VMEM((chunks, lags, GROUP), f32),
            pltpu.VMEM((chunks, lags, GROUP), f32),
            pltpu.VMEM((n_ch, chunks, lags, GROUP), f32),
            pltpu.VMEM((n_ctx, chunks, lags, GROUP), f32),
            pltpu.SemaphoreType.DMA((4, chunks)),
            pltpu.SemaphoreType.DMA((4, chunks)),
            pltpu.SemaphoreType.DMA((4, chunks)),
            pltpu.SemaphoreType.DMA((4, chunks)),
            pltpu.SemaphoreType.DMA((2, n_ch)),
            pltpu.SemaphoreType.DMA((2, n_ch)),
            pltpu.SemaphoreType.DMA((2, n_ctx)),
            pltpu.SemaphoreType.DMA((2, n_ctx)),
            pltpu.SemaphoreType.DMA((2, 2, chunks)),
            pltpu.SemaphoreType.DMA((chunks,)),
            pltpu.SemaphoreType.DMA((2, 2, chunks)),
        ],
        compiler_params=pltpu.CompilerParams(
            collective_id=0, has_side_effects=True, vmem_limit_bytes=56 * 2**20
        ),
        cost_estimate=pl.CostEstimate(
            flops=6 * rows * rows * own * lags * half,
            bytes_accessed=10 * slots * rows * channels,
            transcendentals=0,
        ),
    )(tile_owner, support.T, conv_input, gate_signal, cotangent, filters)
    gate_grad = (cotangent.astype(f32) * conv.astype(f32)).astype(bf16)
    return gate_grad, input_grad, filter_grad


def solution(mesh):
    return jax.shard_map(
        per_device,
        mesh=mesh,
        in_specs=(P("ctx", None, "ch"), P("ctx", None, "ch"), P("ctx", None, "ch"), P(), P(), P()),
        out_specs=(P("ctx", None, "ch"), P("ctx", None, "ch"), P()),
        check_vma=False,
    )
```

```python
import functools
import math

import jax
import jax.numpy as jnp
from jax import lax
from jax.experimental import pallas as pl
from jax.experimental.pallas import tpu as pltpu
from jax.sharding import PartitionSpec as P

GROUP = 128
LEAD = 8
LAG = 5
LATE = 2
LO = 4
MESH = pl.DeviceIdType.MESH


def copy_to(src, dst, send, recv, to, axis="ctx"):
    return pltpu.make_async_remote_copy(
        src_ref=src,
        dst_ref=dst,
        send_sem=send,
        recv_sem=recv,
        device_id={axis: to},
        device_id_type=MESH,
    )


def kernel(
    n_ctx,
    n_ch,
    norm,
    owner_ref,
    support_ref,
    x_ref,
    gate_ref,
    cot_ref,
    taps_ref,
    gg_ref,
    ig_ref,
    fg_ref,
    xo,
    gate_own,
    gate_far,
    cot_own,
    cot_far,
    gg_own,
    gg_far,
    ig_own,
    xr,
    wr,
    ws,
    hx,
    gw,
    sx,
    tw,
    rc,
    ra,
    sc,
    sa,
    cx,
    cw,
    mat_a,
    mat_b,
    rhs,
    vv,
    co,
    ao,
    tab,
    taps,
    fmask_ref,
    bmask_ref,
    sums,
    ch_sums,
    ch_got,
    ctx_got,
    y_send,
    y_recv,
    z_send,
    z_recv,
    ch_send,
    ch_recv,
    ctx_send,
    ctx_recv,
    in_sem,
    x_sem,
    out_sem,
):
    slots, rows, channels = x_ref.shape
    half = channels // 2
    chunks = half // GROUP
    lags = support_ref.shape[0]
    total = owner_ref.shape[0]
    own = 2 * slots
    reach = lags - 1
    f32, bf16 = jnp.float32, jnp.bfloat16
    me = lax.axis_index("ctx")
    pair = me // 2
    side = me % 2
    partner = me + 1 - 2 * side
    up, down = me + 2, me - 2
    has_up = pair < n_ctx // 2 - 1
    has_down = pair > 0
    t_s, t_t, t_w, t_v, t_mine, t_theirs = 0, 7, 14, 29, 44, 48

    my_ch = lax.axis_index("ch")
    batches = [(0, chunks - LATE), (chunks - LATE, LATE)]

    def other(d, axis, mine, size):
        return {axis: lax.rem(mine + d, size)}

    def lanes(which, c):
        return pl.ds(pl.multiple_of(which * half + c * GROUP, GROUP), GROUP)

    def load(kind, which, c):
        src = (gate_ref, cot_ref)[kind]
        at = 0 if which is side else 1
        dst = ((gate_own, gate_far), (cot_own, cot_far))[kind][at]
        return pltpu.make_async_copy(
            src.at[:, :, lanes(which, c)], dst.at[c], in_sem.at[kind, at, c]
        )

    def load_x(c):
        return pltpu.make_async_copy(x_ref.at[:, :, lanes(side, c)], xo.at[c], x_sem.at[c])

    def store(kind, which, c):
        dst = (gg_ref, ig_ref)[kind].at[:, :, lanes(which, c)]
        if which is side:
            src = (gg_own, ig_own)[kind].at[c]
        else:
            src = (gg_far, ra)[kind].at[c]
        at = 0 if which is side else 1
        return pltpu.make_async_copy(src, dst, out_sem.at[kind, at, c])

    far = 1 - side

    @pl.loop(0, chunks)
    def _(c):
        load(0, far, c).start()
        load(1, far, c).start()
        load_x(c).start()
        load(0, side, c).start()
        load(1, side, c).start()

    barrier = pltpu.get_barrier_semaphore()

    @pl.loop(1, n_ctx)
    def _(d):
        pl.semaphore_signal(
            barrier, inc=1, device_id=other(d, "ctx", me, n_ctx), device_id_type=MESH
        )

    @pl.loop(1, n_ch)
    def _(d):
        pl.semaphore_signal(
            barrier, inc=1, device_id=other(d, "ch", my_ch, n_ch), device_id_type=MESH
        )

    pl.semaphore_wait(barrier, n_ctx + n_ch - 2)

    co[own] = jnp.zeros((rows, GROUP), f32)
    ao[own] = jnp.zeros((rows, GROUP), f32)

    @pl.when(jnp.logical_not(has_down))
    def _():
        hx[...] = jnp.zeros(hx.shape, bf16)

    @pl.when(jnp.logical_not(has_up))
    def _():
        gw[...] = jnp.zeros(gw.shape, bf16)

    def x_copy(c):
        return copy_to(
            x_ref.at[:, :, lanes(far, c)], xr.at[c], y_send.at[0, c], y_recv.at[0, c], partner
        )

    def w_copy(c):
        return copy_to(ws.at[c], wr.at[c], y_send.at[1, c], y_recv.at[1, c], partner)

    def c_copy(c):
        return copy_to(sc.at[c], rc.at[c], y_send.at[2, c], y_recv.at[2, c], partner)

    def a_copy(c):
        return copy_to(sa.at[c], ra.at[c], y_send.at[3, c], y_recv.at[3, c], partner)

    def x_up(c, part):
        span = pl.ds(0, LO) if part == 0 else pl.ds(LO, reach - LO)
        return copy_to(
            sx.at[c, span], hx.at[c, span], z_send.at[part, c], z_recv.at[part, c], up
        )

    def w_down(c, part):
        span = pl.ds(0, LO) if part == 0 else pl.ds(LO, reach - LO)
        return copy_to(
            tw.at[c, span], gw.at[c, span], z_send.at[2 + part, c], z_recv.at[2 + part, c], down
        )

    def weigh(j, which, c):
        gate, cot = (gate_own, cot_own) if which is side else (gate_far, cot_far)
        return (gate[c, j].astype(f32) * cot[c, j].astype(f32)).astype(bf16)

    def launch(c):
        x_copy(c).start()
        load(0, far, c).wait()
        load(1, far, c).wait()
        for j in range(slots):
            ws[c, j] = weigh(j, far, c)
        w_copy(c).start()

    def send_halo(c, part):
        for q in range(LO) if part == 0 else range(LO, reach):
            sx[c, q] = cx[c, tab[t_s + q]]
            tw[c, q] = cw[c, tab[t_t + q]]

        @pl.when(has_up)
        def _():
            x_up(c, part).start()

        @pl.when(has_down)
        def _():
            w_down(c, part).start()

    def take_halo(c, part):
        @pl.when(has_down)
        def _():
            x_up(c, part).wait_recv()

        @pl.when(has_up)
        def _():
            w_down(c, part).wait_recv()

        for q in range(LO) if part == 0 else range(LO, reach):
            cx[c, own + q] = hx[c, q]
            cw[c, own + q] = gw[c, q]

    def gather_pair(c):
        mine, theirs = side * slots, far * slots
        load_x(c).wait()
        load(0, side, c).wait()
        load(1, side, c).wait()
        for j in range(slots):
            cx[c, mine + j] = xo[c, j]
            cw[c, mine + j] = weigh(j, side, c)
        x_copy(c).wait_recv()
        w_copy(c).wait_recv()
        for j in range(slots):
            cx[c, theirs + j] = xr[c, j]
            cw[c, theirs + j] = wr[c, j]
        send_halo(c, 0)

    def relay(c):
        take_halo(c, 0)
        send_halo(c, 1)

    def work(c):
        row = lax.broadcasted_iota(jnp.int32, (rows, GROUP), 0)
        lane = lax.broadcasted_iota(jnp.int32, (rows, GROUP), 1)
        upper = lane >= row
        before = jnp.zeros((rows, GROUP), f32)
        for k in range(lags):
            now = pltpu.roll(
                jnp.broadcast_to(taps[c, k : k + 1, :], (rows, GROUP)),
                0, 1, stride=1, stride_axis=0,
            )
            block = jnp.where(upper, now, before)
            at = pl.ds((lags - 1 - k) * GROUP, GROUP)
            mat_a[:, at] = block.T.astype(bf16)
            mat_b[:, pl.ds(k * GROUP, GROUP)] = block.astype(bf16)
            before = now

        take_halo(c, 1)

        def fill(cur, base, mask):
            for r in range(own + reach):
                tile = cur[c, tab[base + r]].reshape(rows // 16, 16, GROUP)
                for u in range(max(0, r - reach), min(own, r + 1)):
                    b = r - u
                    masked = tile * mask[u * lags + b][None]
                    rhs[pl.ds(b * rows, rows), pl.ds(u * GROUP, GROUP)] = masked.reshape(rows, GROUP)

        fill(cw, t_v, bmask_ref)
        out = jnp.dot(mat_b[...], rhs[...], preferred_element_type=f32)
        for u in range(own):
            ao[u] = out[:, u * GROUP : (u + 1) * GROUP]
            vv[:, pl.ds(u * GROUP, GROUP)] = cw[c, tab[t_v + u]]
        for j in range(slots):
            sa[c, j] = ao[tab[t_theirs + j]].astype(bf16)
        a_copy(c).start()
        for j in range(slots):
            ig_own[c, j] = ao[tab[t_mine + j]].astype(bf16)
        store(1, side, c).start()
        fill(cx, t_w, fmask_ref)
        out = jnp.dot(mat_a[...], rhs[...], preferred_element_type=f32)
        for u in range(own):
            co[u] = out[:, u * GROUP : (u + 1) * GROUP]
        for j in range(slots):
            sc[c, j] = co[tab[t_theirs + j]].astype(bf16)
        c_copy(c).start()
        for j in range(slots):
            gg_own[c, j] = (cot_own[c, j].astype(f32) * co[tab[t_mine + j]]).astype(bf16)
        store(0, side, c).start()
        flip = (row + lane == rows - 1).astype(f32).astype(bf16)
        turned = jnp.dot(flip, vv[...], preferred_element_type=f32).astype(bf16)
        square = lax.dot_general(
            turned, rhs[...], (((1,), (1,)), ((), ())), preferred_element_type=f32
        )
        for k in range(lags):
            here = square[:, (lags - 1 - k) * rows : (lags - k) * rows]
            if k < lags - 1:
                above = square[:, (lags - 2 - k) * rows : (lags - 1 - k) * rows]
            else:
                above = jnp.zeros_like(here)
            skewed = pltpu.roll(
                jnp.where(row + lane <= rows - 1, here, above), 0, 1, stride=1, stride_axis=0
            )
            sums[c, k : k + 1, :] = jnp.sum(skewed, axis=0, keepdims=True)

    def finish(c):
        a_copy(c).wait_recv()
        store(1, far, c).start()
        c_copy(c).wait_recv()
        for j in range(slots):
            gg_far[c, j] = (cot_far[c, j].astype(f32) * rc[c, j].astype(f32)).astype(bf16)
        store(0, far, c).start()

    def over_ch(b, d, sender):
        start, size = batches[b]
        return copy_to(
            sums.at[pl.ds(start, size)],
            ch_got.at[sender, pl.ds(start, size)],
            ch_send.at[b, d],
            ch_recv.at[b, sender],
            lax.rem(my_ch + d, n_ch),
            "ch",
        )

    def over_ctx(b, d, sender):
        start, size = batches[b]
        return copy_to(
            ch_sums.at[pl.ds(start, size)],
            ctx_got.at[sender, pl.ds(start, size)],
            ctx_send.at[b, d],
            ctx_recv.at[b, sender],
            lax.rem(me + d, n_ctx),
        )

    def sum_over_ch(b):
        @pl.loop(1, n_ch)
        def _(d):
            over_ch(b, d, my_ch).start()

        at = pl.ds(*batches[b])
        ch_got[my_ch, at] = sums[at]

    def sum_over_ctx(b):
        @pl.loop(1, n_ch)
        def _(d):
            over_ch(b, d, lax.rem(my_ch + d, n_ch)).wait_recv()

        at = pl.ds(*batches[b])
        acc = ch_got[0, at]
        for i in range(1, n_ch):
            acc = acc + ch_got[i, at]
        ch_sums[at] = acc

        @pl.loop(1, n_ctx)
        def _(d):
            over_ctx(b, d, me).start()

        ctx_got[me, at] = acc

    def end_sums():
        for b in range(2):
            @pl.loop(1, n_ctx)
            def _(d):
                over_ctx(b, d, lax.rem(me + d, n_ctx)).wait_recv()

        row = lax.broadcasted_iota(jnp.int32, (GROUP, GROUP), 0)
        lane = lax.broadcasted_iota(jnp.int32, (GROUP, GROUP), 1)
        flip = (row + lane == GROUP - 1).astype(f32)
        for parity in range(2):
            acc = lax.fori_loop(
                1,
                n_ctx // 2,
                lambda i, acc: acc + ctx_got[2 * i + parity],
                ctx_got[parity],
            )
            flat = jnp.dot(
                acc.reshape(chunks * lags, GROUP),
                flip,
                preferred_element_type=f32,
                precision=lax.Precision.HIGHEST,
            )
            whole = flat.reshape(chunks, lags, GROUP) * norm
            for c in range(chunks):
                for k in range(lags):
                    fg_ref[
                        parity * chunks + c : parity * chunks + c + 1,
                        k * GROUP : (k + 1) * GROUP,
                    ] = whole[c, k : k + 1]

    def make_tables():
        def count(t, found):
            holder = owner_ref[t]
            one = lambda hit: hit.astype(jnp.int32)
            return (
                found[0] + one(holder == 2 * pair),
                found[1] + one(holder == 2 * pair + 1),
                found[2] + one(holder < 2 * pair),
            )

        zero = jnp.int32(0)
        count0, count1, first = lax.fori_loop(0, total, count, (zero, zero, zero))
        n = count0 + count1

        mine = taps_ref[pl.ds(pl.multiple_of(side * chunks, chunks), chunks), :]
        mine = mine.astype(bf16).astype(f32)
        for c in range(chunks):
            for k in range(lags):
                taps[c, k : k + 1, :] = mine[c : c + 1, k * GROUP : (k + 1) * GROUP]

        def place(u):
            return jnp.clip(jnp.where(u < count0, u, slots + u - count0), 0, own - 1)

        def beyond(q):
            return jnp.clip(own + q - n, 0, own + reach - 1)

        for q in range(reach):
            tab[t_s + q] = jnp.where(q < n, place(n - 1 - q), beyond(q))
            tab[t_t + q] = jnp.where(q < n, place(q), beyond(q))
        for r in range(own + reach):
            tab[t_w + r] = own + reach - 1 - r if r < reach else place(r - reach)
            tab[t_v + r] = jnp.where(r < n, place(r), beyond(r))
        for j in range(slots):
            at0 = jnp.where(j < count0, j, own)
            at1 = jnp.where(j < count1, j + count0, own)
            tab[t_mine + j] = jnp.where(side == 0, at0, at1)
            tab[t_theirs + j] = jnp.where(side == 0, at1, at0)

        def put(mask, at, ok):
            value = ok.astype(jnp.int32).astype(f32)
            mask[at] = jnp.full((16, GROUP), value, f32).astype(bf16)

        for u in range(own):
            for k in range(lags):
                live = u < n
                found = support_ref[k, jnp.clip(first + u, 0, total - 1)] >= 0
                put(fmask_ref, u * lags + lags - 1 - k, live & found)
                later = first + u + k
                found = support_ref[k, jnp.clip(later, 0, total - 1)] >= 0
                put(bmask_ref, u * lags + k, live & found & (later < total))

    for c in range(min(LEAD, chunks)):
        launch(c)
    make_tables()

    @pl.loop(0, chunks + LAG)
    def _(s):
        if LEAD < chunks:
            @pl.when(s + LEAD < chunks)
            def _():
                launch(s + LEAD)

        @pl.when(s < chunks)
        def _():
            gather_pair(s)

        @pl.when((s >= 1) & (s < chunks + 1))
        def _():
            relay(s - 1)

        @pl.when((s >= 2) & (s < chunks + 2))
        def _():
            work(s - 2)

        for b, (start, size) in enumerate(batches):
            @pl.when(s == start + size + 1)
            def _():
                sum_over_ch(b)

            @pl.when(s == start + size + 2)
            def _():
                sum_over_ctx(b)

        @pl.when(s == chunks + 3)
        def _():
            end_sums()

        @pl.when(s >= LAG)
        def _():
            finish(s - LAG)

    for b in range(2):
        @pl.loop(1, n_ch)
        def _(d):
            over_ch(b, d, my_ch).wait_send()

        @pl.loop(1, n_ctx)
        def _(d):
            over_ctx(b, d, me).wait_send()

    @pl.loop(0, chunks)
    def _(c):
        for kind in range(2):
            store(kind, side, c).wait()
            store(kind, far, c).wait()
        x_copy(c).wait_send()
        w_copy(c).wait_send()
        a_copy(c).wait_send()
        c_copy(c).wait_send()

        @pl.when(has_up)
        def _():
            x_up(c, 0).wait_send()
            x_up(c, 1).wait_send()

        @pl.when(has_down)
        def _():
            w_down(c, 0).wait_send()
            w_down(c, 1).wait_send()


def hand_over(slots, gg_in, ig_in, fg_in, gg_out, ig_out, fg_out, sem, fg_sem):
    rows = gg_in.shape[1] // 2
    copies = [pltpu.make_async_copy(fg_in, fg_out, fg_sem)]
    for kind, (src, dst) in enumerate(((gg_in, gg_out), (ig_in, ig_out))):
        for j in range(slots):
            for part in range(2):
                at = (j, pl.ds(part * rows, rows))
                copies.append(
                    pltpu.make_async_copy(src.at[at], dst.at[at], sem.at[kind, j, part])
                )
    for copy in copies:
        copy.start()
    for copy in copies:
        copy.wait()


def per_device(conv_input, gate_signal, cotangent, filters, tile_owner, support):
    slots, rows, channels = conv_input.shape
    lags = support.shape[1]
    filter_count, taps = filters.shape
    n_ctx = lax.axis_size("ctx")
    n_ch = lax.axis_size("ch")
    half = channels // 2
    chunks = half // GROUP
    own, reach = 2 * slots, lags - 1
    norm = 1.0 / math.sqrt(
        tile_owner.shape[0] * rows * channels * lax.axis_size("ch") / filter_count
    )
    bf16, f32 = jnp.bfloat16, jnp.float32
    vmem = pl.BlockSpec(memory_space=pltpu.VMEM)
    whole = jax.ShapeDtypeStruct(conv_input.shape, bf16)
    part = lambda count: pltpu.VMEM((chunks, count, rows, GROUP), bf16)
    hbm = pl.BlockSpec(memory_space=pl.ANY)
    results = pl.pallas_call(
        functools.partial(kernel, n_ctx, n_ch, norm),
        out_shape=(whole, whole, jax.ShapeDtypeStruct(filters.shape, f32)),
        in_specs=[pl.BlockSpec(memory_space=pltpu.SMEM)] * 2 + [hbm] * 3 + [vmem],
        out_specs=(hbm, hbm, vmem),
        scratch_shapes=[
            part(slots),
            part(slots),
            part(slots),
            part(slots),
            part(slots),
            part(slots),
            part(slots),
            part(slots),
            part(slots),
            part(slots),
            part(slots),
            part(reach),
            part(reach),
            part(reach),
            part(reach),
            part(slots),
            part(slots),
            part(slots),
            part(slots),
            part(own + reach),
            part(own + reach),
            pltpu.VMEM((rows, lags * rows), bf16),
            pltpu.VMEM((rows, lags * rows), bf16),
            pltpu.VMEM((lags * rows, own * GROUP), bf16),
            pltpu.VMEM((rows, own * GROUP), bf16),
            pltpu.VMEM((own + 1, rows, GROUP), f32),
            pltpu.VMEM((own + 1, rows, GROUP), f32),
            pltpu.SMEM((52,), jnp.int32),
            pltpu.VMEM((chunks, lags, GROUP), f32),
            pltpu.VMEM((own * lags, 16, GROUP), bf16),
            pltpu.VMEM((own * lags, 16, GROUP), bf16),
            pltpu.VMEM((chunks, lags, GROUP), f32),
            pltpu.VMEM((chunks, lags, GROUP), f32),
            pltpu.VMEM((n_ch, chunks, lags, GROUP), f32),
            pltpu.VMEM((n_ctx, chunks, lags, GROUP), f32),
            pltpu.SemaphoreType.DMA((4, chunks)),
            pltpu.SemaphoreType.DMA((4, chunks)),
            pltpu.SemaphoreType.DMA((4, chunks)),
            pltpu.SemaphoreType.DMA((4, chunks)),
            pltpu.SemaphoreType.DMA((2, n_ch)),
            pltpu.SemaphoreType.DMA((2, n_ch)),
            pltpu.SemaphoreType.DMA((2, n_ctx)),
            pltpu.SemaphoreType.DMA((2, n_ctx)),
            pltpu.SemaphoreType.DMA((2, 2, chunks)),
            pltpu.SemaphoreType.DMA((chunks,)),
            pltpu.SemaphoreType.DMA((2, 2, chunks)),
        ],
        compiler_params=pltpu.CompilerParams(
            collective_id=0, has_side_effects=True, vmem_limit_bytes=56 * 2**20
        ),
        cost_estimate=pl.CostEstimate(
            flops=6 * rows * rows * own * lags * half,
            bytes_accessed=10 * slots * rows * channels,
            transcendentals=0,
        ),
    )(tile_owner, support.T, conv_input, gate_signal, cotangent, filters)
    return pl.pallas_call(
        functools.partial(hand_over, slots),
        out_shape=(whole, whole, jax.ShapeDtypeStruct(filters.shape, f32)),
        in_specs=[hbm] * 3,
        out_specs=(hbm,) * 3,
        scratch_shapes=[pltpu.SemaphoreType.DMA((2, slots, 2)), pltpu.SemaphoreType.DMA],
        compiler_params=pltpu.CompilerParams(vmem_limit_bytes=60 * 2**20),
        cost_estimate=pl.CostEstimate(
            flops=0, bytes_accessed=8 * slots * rows * channels, transcendentals=0
        ),
    )(*results)


def solution(mesh):
    return jax.shard_map(
        per_device,
        mesh=mesh,
        in_specs=(P("ctx", None, "ch"), P("ctx", None, "ch"), P("ctx", None, "ch"), P(), P(), P()),
        out_specs=(P("ctx", None, "ch"), P("ctx", None, "ch"), P()),
        check_vma=False,
    )
```

```python
import functools
import math

import jax
import jax.numpy as jnp
from jax import lax
from jax.experimental import pallas as pl
from jax.experimental.pallas import tpu as pltpu
from jax.sharding import PartitionSpec as P

GROUP = 128
LEAD = 8
LAG = 5
LATE = 2
LO = 4
MESH = pl.DeviceIdType.MESH


def copy_to(src, dst, send, recv, to, axis="ctx"):
    return pltpu.make_async_remote_copy(
        src_ref=src,
        dst_ref=dst,
        send_sem=send,
        recv_sem=recv,
        device_id={axis: to},
        device_id_type=MESH,
    )


def kernel(
    n_ctx,
    n_ch,
    norm,
    owner_ref,
    support_ref,
    x_ref,
    gate_ref,
    cot_ref,
    taps_ref,
    gg_ref,
    ig_ref,
    fg_ref,
    xo,
    gate_own,
    gate_far,
    cot_own,
    cot_far,
    gg_own,
    gg_far,
    ig_own,
    xr,
    wr,
    ws,
    hx,
    gw,
    sx,
    tw,
    rc,
    ra,
    sc,
    sa,
    cx,
    cw,
    mat_a,
    mat_b,
    rhs,
    vv,
    co,
    ao,
    tab,
    taps,
    fmask_ref,
    bmask_ref,
    sums,
    ch_sums,
    ch_got,
    ctx_got,
    y_send,
    y_recv,
    z_send,
    z_recv,
    ch_send,
    ch_recv,
    ctx_send,
    ctx_recv,
    in_sem,
    x_sem,
    out_sem,
):
    slots, rows, channels = x_ref.shape
    half = channels // 2
    chunks = half // GROUP
    lags = support_ref.shape[0]
    total = owner_ref.shape[0]
    own = 2 * slots
    reach = lags - 1
    f32, bf16 = jnp.float32, jnp.bfloat16
    me = lax.axis_index("ctx")
    pair = me // 2
    side = me % 2
    partner = me + 1 - 2 * side
    up, down = me + 2, me - 2
    has_up = pair < n_ctx // 2 - 1
    has_down = pair > 0
    t_s, t_t, t_w, t_v, t_mine, t_theirs = 0, 7, 14, 29, 44, 48

    my_ch = lax.axis_index("ch")
    batches = [(0, chunks - LATE), (chunks - LATE, LATE)]

    def other(d, axis, mine, size):
        return {axis: lax.rem(mine + d, size)}

    def lanes(which, c):
        return pl.ds(pl.multiple_of(which * half + c * GROUP, GROUP), GROUP)

    def load(kind, which, c):
        src = (gate_ref, cot_ref)[kind]
        at = 0 if which is side else 1
        dst = ((gate_own, gate_far), (cot_own, cot_far))[kind][at]
        return pltpu.make_async_copy(
            src.at[:, :, lanes(which, c)], dst.at[c], in_sem.at[kind, at, c]
        )

    def load_x(c):
        return pltpu.make_async_copy(x_ref.at[:, :, lanes(side, c)], xo.at[c], x_sem.at[c])

    def store(kind, which, c):
        dst = (gg_ref, ig_ref)[kind].at[:, :, lanes(which, c)]
        if which is side:
            src = (gg_own, ig_own)[kind].at[c]
        else:
            src = (gg_far, ra)[kind].at[c]
        at = 0 if which is side else 1
        return pltpu.make_async_copy(src, dst, out_sem.at[kind, at, c])

    far = 1 - side

    @pl.loop(0, chunks)
    def _(c):
        load(0, far, c).start()
        load(1, far, c).start()
        load_x(c).start()
        load(0, side, c).start()
        load(1, side, c).start()

    barrier = pltpu.get_barrier_semaphore()

    @pl.loop(1, n_ctx)
    def _(d):
        pl.semaphore_signal(
            barrier, inc=1, device_id=other(d, "ctx", me, n_ctx), device_id_type=MESH
        )

    @pl.loop(1, n_ch)
    def _(d):
        pl.semaphore_signal(
            barrier, inc=1, device_id=other(d, "ch", my_ch, n_ch), device_id_type=MESH
        )

    pl.semaphore_wait(barrier, n_ctx + n_ch - 2)

    co[own] = jnp.zeros((rows, GROUP), f32)
    ao[own] = jnp.zeros((rows, GROUP), f32)

    @pl.when(jnp.logical_not(has_down))
    def _():
        hx[...] = jnp.zeros(hx.shape, bf16)

    @pl.when(jnp.logical_not(has_up))
    def _():
        gw[...] = jnp.zeros(gw.shape, bf16)

    def x_copy(c):
        return copy_to(
            x_ref.at[:, :, lanes(far, c)], xr.at[c], y_send.at[0, c], y_recv.at[0, c], partner
        )

    def w_copy(c):
        return copy_to(ws.at[c], wr.at[c], y_send.at[1, c], y_recv.at[1, c], partner)

    def c_copy(c):
        return copy_to(sc.at[c], rc.at[c], y_send.at[2, c], y_recv.at[2, c], partner)

    def a_copy(c):
        return copy_to(sa.at[c], ra.at[c], y_send.at[3, c], y_recv.at[3, c], partner)

    def x_up(c, part):
        span = pl.ds(0, LO) if part == 0 else pl.ds(LO, reach - LO)
        return copy_to(
            sx.at[c, span], hx.at[c, span], z_send.at[part, c], z_recv.at[part, c], up
        )

    def w_down(c, part):
        span = pl.ds(0, LO) if part == 0 else pl.ds(LO, reach - LO)
        return copy_to(
            tw.at[c, span], gw.at[c, span], z_send.at[2 + part, c], z_recv.at[2 + part, c], down
        )

    def weigh(j, which, c):
        gate, cot = (gate_own, cot_own) if which is side else (gate_far, cot_far)
        return (gate[c, j].astype(f32) * cot[c, j].astype(f32)).astype(bf16)

    def launch(c):
        x_copy(c).start()
        load(0, far, c).wait()
        load(1, far, c).wait()
        for j in range(slots):
            ws[c, j] = weigh(j, far, c)
        w_copy(c).start()

    def send_halo(c, part):
        for q in range(LO) if part == 0 else range(LO, reach):
            sx[c, q] = cx[c, tab[t_s + q]]
            tw[c, q] = cw[c, tab[t_t + q]]

        @pl.when(has_up)
        def _():
            x_up(c, part).start()

        @pl.when(has_down)
        def _():
            w_down(c, part).start()

    def take_halo(c, part):
        @pl.when(has_down)
        def _():
            x_up(c, part).wait_recv()

        @pl.when(has_up)
        def _():
            w_down(c, part).wait_recv()

        for q in range(LO) if part == 0 else range(LO, reach):
            cx[c, own + q] = hx[c, q]
            cw[c, own + q] = gw[c, q]

    def gather_pair(c):
        mine, theirs = side * slots, far * slots
        load_x(c).wait()
        load(0, side, c).wait()
        load(1, side, c).wait()
        for j in range(slots):
            cx[c, mine + j] = xo[c, j]
            cw[c, mine + j] = weigh(j, side, c)
        x_copy(c).wait_recv()
        w_copy(c).wait_recv()
        for j in range(slots):
            cx[c, theirs + j] = xr[c, j]
            cw[c, theirs + j] = wr[c, j]
        send_halo(c, 0)

    def relay(c):
        take_halo(c, 0)
        send_halo(c, 1)

    def work(c):
        row = lax.broadcasted_iota(jnp.int32, (rows, GROUP), 0)
        lane = lax.broadcasted_iota(jnp.int32, (rows, GROUP), 1)
        upper = lane >= row
        before = jnp.zeros((rows, GROUP), f32)
        for k in range(lags):
            now = pltpu.roll(
                jnp.broadcast_to(taps[c, k : k + 1, :], (rows, GROUP)),
                0, 1, stride=1, stride_axis=0,
            )
            block = jnp.where(upper, now, before)
            at = pl.ds((lags - 1 - k) * GROUP, GROUP)
            mat_a[:, at] = block.T.astype(bf16)
            mat_b[:, pl.ds(k * GROUP, GROUP)] = block.astype(bf16)
            before = now

        take_halo(c, 1)

        def fill(cur, base, mask):
            for r in range(own + reach):
                tile = cur[c, tab[base + r]].reshape(rows // 16, 16, GROUP)
                for u in range(max(0, r - reach), min(own, r + 1)):
                    b = r - u
                    masked = tile * mask[u * lags + b][None]
                    rhs[pl.ds(b * rows, rows), pl.ds(u * GROUP, GROUP)] = masked.reshape(rows, GROUP)

        fill(cw, t_v, bmask_ref)
        out = jnp.dot(mat_b[...], rhs[...], preferred_element_type=f32)
        for u in range(own):
            ao[u] = out[:, u * GROUP : (u + 1) * GROUP]
            vv[:, pl.ds(u * GROUP, GROUP)] = cw[c, tab[t_v + u]]
        for j in range(slots):
            sa[c, j] = ao[tab[t_theirs + j]].astype(bf16)
        a_copy(c).start()
        for j in range(slots):
            ig_own[c, j] = ao[tab[t_mine + j]].astype(bf16)
        store(1, side, c).start()
        fill(cx, t_w, fmask_ref)
        out = jnp.dot(mat_a[...], rhs[...], preferred_element_type=f32)
        for u in range(own):
            co[u] = out[:, u * GROUP : (u + 1) * GROUP]
        for j in range(slots):
            sc[c, j] = co[tab[t_theirs + j]].astype(bf16)
        c_copy(c).start()
        for j in range(slots):
            gg_own[c, j] = (cot_own[c, j].astype(f32) * co[tab[t_mine + j]]).astype(bf16)
        store(0, side, c).start()
        flip = (row + lane == rows - 1).astype(f32).astype(bf16)
        turned = jnp.dot(flip, vv[...], preferred_element_type=f32).astype(bf16)
        square = lax.dot_general(
            turned, rhs[...], (((1,), (1,)), ((), ())), preferred_element_type=f32
        )
        for k in range(lags):
            here = square[:, (lags - 1 - k) * rows : (lags - k) * rows]
            if k < lags - 1:
                above = square[:, (lags - 2 - k) * rows : (lags - 1 - k) * rows]
            else:
                above = jnp.zeros_like(here)
            skewed = pltpu.roll(
                jnp.where(row + lane <= rows - 1, here, above), 0, 1, stride=1, stride_axis=0
            )
            sums[c, k : k + 1, :] = jnp.sum(skewed, axis=0, keepdims=True)

    def finish(c):
        a_copy(c).wait_recv()
        store(1, far, c).start()
        c_copy(c).wait_recv()
        for j in range(slots):
            gg_far[c, j] = (cot_far[c, j].astype(f32) * rc[c, j].astype(f32)).astype(bf16)
        store(0, far, c).start()

    def over_ch(b, d, sender):
        start, size = batches[b]
        return copy_to(
            sums.at[pl.ds(start, size)],
            ch_got.at[sender, pl.ds(start, size)],
            ch_send.at[b, d],
            ch_recv.at[b, sender],
            lax.rem(my_ch + d, n_ch),
            "ch",
        )

    def over_ctx(b, d, sender):
        start, size = batches[b]
        return copy_to(
            ch_sums.at[pl.ds(start, size)],
            ctx_got.at[sender, pl.ds(start, size)],
            ctx_send.at[b, d],
            ctx_recv.at[b, sender],
            lax.rem(me + d, n_ctx),
        )

    def sum_over_ch(b):
        @pl.loop(1, n_ch)
        def _(d):
            over_ch(b, d, my_ch).start()

        at = pl.ds(*batches[b])
        ch_got[my_ch, at] = sums[at]

    def sum_over_ctx(b):
        @pl.loop(1, n_ch)
        def _(d):
            over_ch(b, d, lax.rem(my_ch + d, n_ch)).wait_recv()

        at = pl.ds(*batches[b])
        acc = ch_got[0, at]
        for i in range(1, n_ch):
            acc = acc + ch_got[i, at]
        ch_sums[at] = acc

        @pl.loop(1, n_ctx)
        def _(d):
            over_ctx(b, d, me).start()

        ctx_got[me, at] = acc

    def end_sums():
        for b in range(2):
            @pl.loop(1, n_ctx)
            def _(d):
                over_ctx(b, d, lax.rem(me + d, n_ctx)).wait_recv()

        row = lax.broadcasted_iota(jnp.int32, (GROUP, GROUP), 0)
        lane = lax.broadcasted_iota(jnp.int32, (GROUP, GROUP), 1)
        flip = (row + lane == GROUP - 1).astype(f32)
        for parity in range(2):
            acc = lax.fori_loop(
                1,
                n_ctx // 2,
                lambda i, acc: acc + ctx_got[2 * i + parity],
                ctx_got[parity],
            )
            flat = jnp.dot(
                acc.reshape(chunks * lags, GROUP),
                flip,
                preferred_element_type=f32,
                precision=lax.Precision.HIGHEST,
            )
            whole = flat.reshape(chunks, lags, GROUP) * norm
            for c in range(chunks):
                for k in range(lags):
                    fg_ref[
                        parity * chunks + c : parity * chunks + c + 1,
                        k * GROUP : (k + 1) * GROUP,
                    ] = whole[c, k : k + 1]

    def make_tables():
        def count(t, found):
            holder = owner_ref[t]
            one = lambda hit: hit.astype(jnp.int32)
            return (
                found[0] + one(holder == 2 * pair),
                found[1] + one(holder == 2 * pair + 1),
                found[2] + one(holder < 2 * pair),
            )

        zero = jnp.int32(0)
        count0, count1, first = lax.fori_loop(0, total, count, (zero, zero, zero))
        n = count0 + count1

        mine = taps_ref[pl.ds(pl.multiple_of(side * chunks, chunks), chunks), :]
        mine = mine.astype(bf16).astype(f32)
        for c in range(chunks):
            for k in range(lags):
                taps[c, k : k + 1, :] = mine[c : c + 1, k * GROUP : (k + 1) * GROUP]

        def place(u):
            return jnp.clip(jnp.where(u < count0, u, slots + u - count0), 0, own - 1)

        def beyond(q):
            return jnp.clip(own + q - n, 0, own + reach - 1)

        for q in range(reach):
            tab[t_s + q] = jnp.where(q < n, place(n - 1 - q), beyond(q))
            tab[t_t + q] = jnp.where(q < n, place(q), beyond(q))
        for r in range(own + reach):
            tab[t_w + r] = own + reach - 1 - r if r < reach else place(r - reach)
            tab[t_v + r] = jnp.where(r < n, place(r), beyond(r))
        for j in range(slots):
            at0 = jnp.where(j < count0, j, own)
            at1 = jnp.where(j < count1, j + count0, own)
            tab[t_mine + j] = jnp.where(side == 0, at0, at1)
            tab[t_theirs + j] = jnp.where(side == 0, at1, at0)

        def put(mask, at, ok):
            value = ok.astype(jnp.int32).astype(f32)
            mask[at] = jnp.full((16, GROUP), value, f32).astype(bf16)

        for u in range(own):
            for k in range(lags):
                live = u < n
                found = support_ref[k, jnp.clip(first + u, 0, total - 1)] >= 0
                put(fmask_ref, u * lags + lags - 1 - k, live & found)
                later = first + u + k
                found = support_ref[k, jnp.clip(later, 0, total - 1)] >= 0
                put(bmask_ref, u * lags + k, live & found & (later < total))

    for c in range(min(LEAD, chunks)):
        launch(c)
    make_tables()

    @pl.loop(0, chunks + LAG)
    def _(s):
        if LEAD < chunks:
            @pl.when(s + LEAD < chunks)
            def _():
                launch(s + LEAD)

        @pl.when(s < chunks)
        def _():
            gather_pair(s)

        @pl.when((s >= 1) & (s < chunks + 1))
        def _():
            relay(s - 1)

        @pl.when((s >= 2) & (s < chunks + 2))
        def _():
            work(s - 2)

        for b, (start, size) in enumerate(batches):
            @pl.when(s == start + size + 1)
            def _():
                sum_over_ch(b)

            @pl.when(s == start + size + 2)
            def _():
                sum_over_ctx(b)

        @pl.when(s == chunks + 3)
        def _():
            end_sums()

        @pl.when(s >= LAG)
        def _():
            finish(s - LAG)

    for b in range(2):
        @pl.loop(1, n_ch)
        def _(d):
            over_ch(b, d, my_ch).wait_send()

        @pl.loop(1, n_ctx)
        def _(d):
            over_ctx(b, d, me).wait_send()

    @pl.loop(0, chunks)
    def _(c):
        for kind in range(2):
            store(kind, side, c).wait()
            store(kind, far, c).wait()
        x_copy(c).wait_send()
        w_copy(c).wait_send()
        a_copy(c).wait_send()
        c_copy(c).wait_send()

        @pl.when(has_up)
        def _():
            x_up(c, 0).wait_send()
            x_up(c, 1).wait_send()

        @pl.when(has_down)
        def _():
            w_down(c, 0).wait_send()
            w_down(c, 1).wait_send()


def hand_over(slots, gg_in, ig_in, fg_in, gg_out, ig_out, fg_out, gg, ig, fg, sem, fg_sem):
    rows = gg_in.shape[1] // 2
    loads = [pltpu.make_async_copy(fg_in, fg, fg_sem.at[0])]
    stores = [pltpu.make_async_copy(fg, fg_out, fg_sem.at[1])]
    for j in range(slots):
        for part in range(2):
            for kind, (src, mid, dst) in enumerate(((gg_in, gg, gg_out), (ig_in, ig, ig_out))):
                at = (j, pl.ds(part * rows, rows))
                sems = sem.at[0, kind, j, part], sem.at[1, kind, j, part]
                loads.append(pltpu.make_async_copy(src.at[at], mid.at[at], sems[0]))
                stores.append(pltpu.make_async_copy(mid.at[at], dst.at[at], sems[1]))
    for load in loads:
        load.start()
    for load, store in zip(loads, stores):
        load.wait()
        store.start()
    for store in stores:
        store.wait()


def per_device(conv_input, gate_signal, cotangent, filters, tile_owner, support):
    slots, rows, channels = conv_input.shape
    lags = support.shape[1]
    filter_count, taps = filters.shape
    n_ctx = lax.axis_size("ctx")
    n_ch = lax.axis_size("ch")
    half = channels // 2
    chunks = half // GROUP
    own, reach = 2 * slots, lags - 1
    norm = 1.0 / math.sqrt(
        tile_owner.shape[0] * rows * channels * lax.axis_size("ch") / filter_count
    )
    bf16, f32 = jnp.bfloat16, jnp.float32
    vmem = pl.BlockSpec(memory_space=pltpu.VMEM)
    whole = jax.ShapeDtypeStruct(conv_input.shape, bf16)
    part = lambda count: pltpu.VMEM((chunks, count, rows, GROUP), bf16)
    hbm = pl.BlockSpec(memory_space=pl.ANY)
    results = pl.pallas_call(
        functools.partial(kernel, n_ctx, n_ch, norm),
        out_shape=(whole, whole, jax.ShapeDtypeStruct(filters.shape, f32)),
        in_specs=[pl.BlockSpec(memory_space=pltpu.SMEM)] * 2 + [hbm] * 3 + [vmem],
        out_specs=(hbm, hbm, vmem),
        scratch_shapes=[
            part(slots),
            part(slots),
            part(slots),
            part(slots),
            part(slots),
            part(slots),
            part(slots),
            part(slots),
            part(slots),
            part(slots),
            part(slots),
            part(reach),
            part(reach),
            part(reach),
            part(reach),
            part(slots),
            part(slots),
            part(slots),
            part(slots),
            part(own + reach),
            part(own + reach),
            pltpu.VMEM((rows, lags * rows), bf16),
            pltpu.VMEM((rows, lags * rows), bf16),
            pltpu.VMEM((lags * rows, own * GROUP), bf16),
            pltpu.VMEM((rows, own * GROUP), bf16),
            pltpu.VMEM((own + 1, rows, GROUP), f32),
            pltpu.VMEM((own + 1, rows, GROUP), f32),
            pltpu.SMEM((52,), jnp.int32),
            pltpu.VMEM((chunks, lags, GROUP), f32),
            pltpu.VMEM((own * lags, 16, GROUP), bf16),
            pltpu.VMEM((own * lags, 16, GROUP), bf16),
            pltpu.VMEM((chunks, lags, GROUP), f32),
            pltpu.VMEM((chunks, lags, GROUP), f32),
            pltpu.VMEM((n_ch, chunks, lags, GROUP), f32),
            pltpu.VMEM((n_ctx, chunks, lags, GROUP), f32),
            pltpu.SemaphoreType.DMA((4, chunks)),
            pltpu.SemaphoreType.DMA((4, chunks)),
            pltpu.SemaphoreType.DMA((4, chunks)),
            pltpu.SemaphoreType.DMA((4, chunks)),
            pltpu.SemaphoreType.DMA((2, n_ch)),
            pltpu.SemaphoreType.DMA((2, n_ch)),
            pltpu.SemaphoreType.DMA((2, n_ctx)),
            pltpu.SemaphoreType.DMA((2, n_ctx)),
            pltpu.SemaphoreType.DMA((2, 2, chunks)),
            pltpu.SemaphoreType.DMA((chunks,)),
            pltpu.SemaphoreType.DMA((2, 2, chunks)),
        ],
        compiler_params=pltpu.CompilerParams(
            collective_id=0, has_side_effects=True, vmem_limit_bytes=56 * 2**20
        ),
        cost_estimate=pl.CostEstimate(
            flops=6 * rows * rows * own * lags * half,
            bytes_accessed=10 * slots * rows * channels,
            transcendentals=0,
        ),
    )(tile_owner, support.T, conv_input, gate_signal, cotangent, filters)
    return pl.pallas_call(
        functools.partial(hand_over, slots),
        out_shape=(whole, whole, jax.ShapeDtypeStruct(filters.shape, f32)),
        in_specs=[hbm] * 3,
        out_specs=(hbm,) * 3,
        scratch_shapes=[
            pltpu.VMEM(conv_input.shape, bf16),
            pltpu.VMEM(conv_input.shape, bf16),
            pltpu.VMEM(filters.shape, f32),
            pltpu.SemaphoreType.DMA((2, 2, slots, 2)),
            pltpu.SemaphoreType.DMA((2,)),
        ],
        compiler_params=pltpu.CompilerParams(vmem_limit_bytes=60 * 2**20),
        cost_estimate=pl.CostEstimate(
            flops=0, bytes_accessed=8 * slots * rows * channels, transcendentals=0
        ),
    )(*results)


def solution(mesh):
    return jax.shard_map(
        per_device,
        mesh=mesh,
        in_specs=(P("ctx", None, "ch"), P("ctx", None, "ch"), P("ctx", None, "ch"), P(), P(), P()),
        out_specs=(P("ctx", None, "ch"), P("ctx", None, "ch"), P()),
        check_vma=False,
    )
```

```python
import functools
import math

import jax
import jax.numpy as jnp
from jax import lax
from jax.experimental import pallas as pl
from jax.experimental.pallas import tpu as pltpu
from jax.sharding import PartitionSpec as P

GROUP = 128
LEAD = 8
LAG = 5
LATE = 2
LO = 4
MESH = pl.DeviceIdType.MESH


def copy_to(src, dst, send, recv, to, axis="ctx"):
    return pltpu.make_async_remote_copy(
        src_ref=src,
        dst_ref=dst,
        send_sem=send,
        recv_sem=recv,
        device_id={axis: to},
        device_id_type=MESH,
    )


def kernel(
    n_ctx,
    n_ch,
    norm,
    owner_ref,
    support_ref,
    x_ref,
    gate_ref,
    cot_ref,
    taps_ref,
    gg_ref,
    ig_ref,
    fg_ref,
    xo,
    xf,
    gate_own,
    gate_far,
    cot_own,
    cot_far,
    gg_own,
    gg_far,
    ig_own,
    xr,
    wr,
    ws,
    hx,
    gw,
    sx,
    tw,
    rc,
    ra,
    sc,
    sa,
    cx,
    cw,
    mat_a,
    mat_b,
    rhs,
    vv,
    co,
    ao,
    tab,
    taps,
    fmask_ref,
    bmask_ref,
    sums,
    ch_sums,
    ch_got,
    ctx_got,
    y_send,
    y_recv,
    z_send,
    z_recv,
    ch_send,
    ch_recv,
    ctx_send,
    ctx_recv,
    in_sem,
    x_sem,
    out_sem,
):
    slots, rows, channels = x_ref.shape
    half = channels // 2
    chunks = half // GROUP
    lags = support_ref.shape[0]
    total = owner_ref.shape[0]
    own = 2 * slots
    reach = lags - 1
    f32, bf16 = jnp.float32, jnp.bfloat16
    me = lax.axis_index("ctx")
    pair = me // 2
    side = me % 2
    partner = me + 1 - 2 * side
    up, down = me + 2, me - 2
    has_up = pair < n_ctx // 2 - 1
    has_down = pair > 0
    t_s, t_t, t_w, t_v, t_mine, t_theirs = 0, 7, 14, 29, 44, 48

    my_ch = lax.axis_index("ch")
    batches = [(0, chunks - LATE), (chunks - LATE, LATE)]

    def other(d, axis, mine, size):
        return {axis: lax.rem(mine + d, size)}

    def lanes(which, c):
        return pl.ds(pl.multiple_of(which * half + c * GROUP, GROUP), GROUP)

    def load(kind, which, c):
        src = (gate_ref, cot_ref)[kind]
        at = 0 if which is side else 1
        dst = ((gate_own, gate_far), (cot_own, cot_far))[kind][at]
        return pltpu.make_async_copy(
            src.at[:, :, lanes(which, c)], dst.at[c], in_sem.at[kind, at, c]
        )

    def load_x(c):
        return pltpu.make_async_copy(x_ref.at[:, :, lanes(side, c)], xo.at[c], x_sem.at[0, c])

    def load_far_x(c):
        return pltpu.make_async_copy(x_ref.at[:, :, lanes(far, c)], xf.at[c], x_sem.at[1, c])

    def store(kind, which, c):
        dst = (gg_ref, ig_ref)[kind].at[:, :, lanes(which, c)]
        if which is side:
            src = (gg_own, ig_own)[kind].at[c]
        else:
            src = (gg_far, ra)[kind].at[c]
        at = 0 if which is side else 1
        return pltpu.make_async_copy(src, dst, out_sem.at[kind, at, c])

    far = 1 - side

    @pl.loop(0, chunks)
    def _(c):
        load_far_x(c).start()
        load(0, far, c).start()
        load(1, far, c).start()
        load_x(c).start()
        load(0, side, c).start()
        load(1, side, c).start()

    barrier = pltpu.get_barrier_semaphore()

    @pl.loop(1, n_ctx)
    def _(d):
        pl.semaphore_signal(
            barrier, inc=1, device_id=other(d, "ctx", me, n_ctx), device_id_type=MESH
        )

    @pl.loop(1, n_ch)
    def _(d):
        pl.semaphore_signal(
            barrier, inc=1, device_id=other(d, "ch", my_ch, n_ch), device_id_type=MESH
        )

    pl.semaphore_wait(barrier, n_ctx + n_ch - 2)

    co[own] = jnp.zeros((rows, GROUP), f32)
    ao[own] = jnp.zeros((rows, GROUP), f32)

    @pl.when(jnp.logical_not(has_down))
    def _():
        hx[...] = jnp.zeros(hx.shape, bf16)

    @pl.when(jnp.logical_not(has_up))
    def _():
        gw[...] = jnp.zeros(gw.shape, bf16)

    def x_copy(c):
        return copy_to(
            xf.at[c], xr.at[c], y_send.at[0, c], y_recv.at[0, c], partner
        )

    def w_copy(c):
        return copy_to(ws.at[c], wr.at[c], y_send.at[1, c], y_recv.at[1, c], partner)

    def c_copy(c):
        return copy_to(sc.at[c], rc.at[c], y_send.at[2, c], y_recv.at[2, c], partner)

    def a_copy(c):
        return copy_to(sa.at[c], ra.at[c], y_send.at[3, c], y_recv.at[3, c], partner)

    def x_up(c, part):
        span = pl.ds(0, LO) if part == 0 else pl.ds(LO, reach - LO)
        return copy_to(
            sx.at[c, span], hx.at[c, span], z_send.at[part, c], z_recv.at[part, c], up
        )

    def w_down(c, part):
        span = pl.ds(0, LO) if part == 0 else pl.ds(LO, reach - LO)
        return copy_to(
            tw.at[c, span], gw.at[c, span], z_send.at[2 + part, c], z_recv.at[2 + part, c], down
        )

    def weigh(j, which, c):
        gate, cot = (gate_own, cot_own) if which is side else (gate_far, cot_far)
        return (gate[c, j].astype(f32) * cot[c, j].astype(f32)).astype(bf16)

    def launch(c):
        load_far_x(c).wait()
        x_copy(c).start()
        load(0, far, c).wait()
        load(1, far, c).wait()
        for j in range(slots):
            ws[c, j] = weigh(j, far, c)
        w_copy(c).start()

    def send_halo(c, part):
        for q in range(LO) if part == 0 else range(LO, reach):
            sx[c, q] = cx[c, tab[t_s + q]]
            tw[c, q] = cw[c, tab[t_t + q]]

        @pl.when(has_up)
        def _():
            x_up(c, part).start()

        @pl.when(has_down)
        def _():
            w_down(c, part).start()

    def take_halo(c, part):
        @pl.when(has_down)
        def _():
            x_up(c, part).wait_recv()

        @pl.when(has_up)
        def _():
            w_down(c, part).wait_recv()

        for q in range(LO) if part == 0 else range(LO, reach):
            cx[c, own + q] = hx[c, q]
            cw[c, own + q] = gw[c, q]

    def gather_pair(c):
        mine, theirs = side * slots, far * slots
        load_x(c).wait()
        load(0, side, c).wait()
        load(1, side, c).wait()
        for j in range(slots):
            cx[c, mine + j] = xo[c, j]
            cw[c, mine + j] = weigh(j, side, c)
        x_copy(c).wait_recv()
        w_copy(c).wait_recv()
        for j in range(slots):
            cx[c, theirs + j] = xr[c, j]
            cw[c, theirs + j] = wr[c, j]
        send_halo(c, 0)

    def relay(c):
        take_halo(c, 0)
        send_halo(c, 1)

    def work(c):
        row = lax.broadcasted_iota(jnp.int32, (rows, GROUP), 0)
        lane = lax.broadcasted_iota(jnp.int32, (rows, GROUP), 1)
        upper = lane >= row
        before = jnp.zeros((rows, GROUP), f32)
        for k in range(lags):
            now = pltpu.roll(
                jnp.broadcast_to(taps[c, k : k + 1, :], (rows, GROUP)),
                0, 1, stride=1, stride_axis=0,
            )
            block = jnp.where(upper, now, before)
            at = pl.ds((lags - 1 - k) * GROUP, GROUP)
            mat_a[:, at] = block.T.astype(bf16)
            mat_b[:, pl.ds(k * GROUP, GROUP)] = block.astype(bf16)
            before = now

        take_halo(c, 1)

        def fill(cur, base, mask):
            for r in range(own + reach):
                tile = cur[c, tab[base + r]].reshape(rows // 16, 16, GROUP)
                for u in range(max(0, r - reach), min(own, r + 1)):
                    b = r - u
                    masked = tile * mask[u * lags + b][None]
                    rhs[pl.ds(b * rows, rows), pl.ds(u * GROUP, GROUP)] = masked.reshape(rows, GROUP)

        fill(cw, t_v, bmask_ref)
        out = jnp.dot(mat_b[...], rhs[...], preferred_element_type=f32)
        for u in range(own):
            ao[u] = out[:, u * GROUP : (u + 1) * GROUP]
            vv[:, pl.ds(u * GROUP, GROUP)] = cw[c, tab[t_v + u]]
        for j in range(slots):
            sa[c, j] = ao[tab[t_theirs + j]].astype(bf16)
        a_copy(c).start()
        for j in range(slots):
            ig_own[c, j] = ao[tab[t_mine + j]].astype(bf16)
        store(1, side, c).start()
        fill(cx, t_w, fmask_ref)
        out = jnp.dot(mat_a[...], rhs[...], preferred_element_type=f32)
        for u in range(own):
            co[u] = out[:, u * GROUP : (u + 1) * GROUP]
        for j in range(slots):
            sc[c, j] = co[tab[t_theirs + j]].astype(bf16)
        c_copy(c).start()
        for j in range(slots):
            gg_own[c, j] = (cot_own[c, j].astype(f32) * co[tab[t_mine + j]]).astype(bf16)
        store(0, side, c).start()
        flip = (row + lane == rows - 1).astype(f32).astype(bf16)
        turned = jnp.dot(flip, vv[...], preferred_element_type=f32).astype(bf16)
        square = lax.dot_general(
            turned, rhs[...], (((1,), (1,)), ((), ())), preferred_element_type=f32
        )
        for k in range(lags):
            here = square[:, (lags - 1 - k) * rows : (lags - k) * rows]
            if k < lags - 1:
                above = square[:, (lags - 2 - k) * rows : (lags - 1 - k) * rows]
            else:
                above = jnp.zeros_like(here)
            skewed = pltpu.roll(
                jnp.where(row + lane <= rows - 1, here, above), 0, 1, stride=1, stride_axis=0
            )
            sums[c, k : k + 1, :] = jnp.sum(skewed, axis=0, keepdims=True)

    def finish(c):
        a_copy(c).wait_recv()
        store(1, far, c).start()
        c_copy(c).wait_recv()
        for j in range(slots):
            gg_far[c, j] = (cot_far[c, j].astype(f32) * rc[c, j].astype(f32)).astype(bf16)
        store(0, far, c).start()

    def over_ch(b, d, sender):
        start, size = batches[b]
        return copy_to(
            sums.at[pl.ds(start, size)],
            ch_got.at[sender, pl.ds(start, size)],
            ch_send.at[b, d],
            ch_recv.at[b, sender],
            lax.rem(my_ch + d, n_ch),
            "ch",
        )

    def over_ctx(b, d, sender):
        start, size = batches[b]
        return copy_to(
            ch_sums.at[pl.ds(start, size)],
            ctx_got.at[sender, pl.ds(start, size)],
            ctx_send.at[b, d],
            ctx_recv.at[b, sender],
            lax.rem(me + d, n_ctx),
        )

    def sum_over_ch(b):
        @pl.loop(1, n_ch)
        def _(d):
            over_ch(b, d, my_ch).start()

        at = pl.ds(*batches[b])
        ch_got[my_ch, at] = sums[at]

    def sum_over_ctx(b):
        @pl.loop(1, n_ch)
        def _(d):
            over_ch(b, d, lax.rem(my_ch + d, n_ch)).wait_recv()

        at = pl.ds(*batches[b])
        acc = ch_got[0, at]
        for i in range(1, n_ch):
            acc = acc + ch_got[i, at]
        ch_sums[at] = acc

        @pl.loop(1, n_ctx)
        def _(d):
            over_ctx(b, d, me).start()

        ctx_got[me, at] = acc

    def end_sums():
        for b in range(2):
            @pl.loop(1, n_ctx)
            def _(d):
                over_ctx(b, d, lax.rem(me + d, n_ctx)).wait_recv()

        row = lax.broadcasted_iota(jnp.int32, (GROUP, GROUP), 0)
        lane = lax.broadcasted_iota(jnp.int32, (GROUP, GROUP), 1)
        flip = (row + lane == GROUP - 1).astype(f32)
        for parity in range(2):
            acc = lax.fori_loop(
                1,
                n_ctx // 2,
                lambda i, acc: acc + ctx_got[2 * i + parity],
                ctx_got[parity],
            )
            flat = jnp.dot(
                acc.reshape(chunks * lags, GROUP),
                flip,
                preferred_element_type=f32,
                precision=lax.Precision.HIGHEST,
            )
            whole = flat.reshape(chunks, lags, GROUP) * norm
            for c in range(chunks):
                for k in range(lags):
                    fg_ref[
                        parity * chunks + c : parity * chunks + c + 1,
                        k * GROUP : (k + 1) * GROUP,
                    ] = whole[c, k : k + 1]

    def make_tables():
        def count(t, found):
            holder = owner_ref[t]
            one = lambda hit: hit.astype(jnp.int32)
            return (
                found[0] + one(holder == 2 * pair),
                found[1] + one(holder == 2 * pair + 1),
                found[2] + one(holder < 2 * pair),
            )

        zero = jnp.int32(0)
        count0, count1, first = lax.fori_loop(0, total, count, (zero, zero, zero))
        n = count0 + count1

        mine = taps_ref[pl.ds(pl.multiple_of(side * chunks, chunks), chunks), :]
        mine = mine.astype(bf16).astype(f32)
        for c in range(chunks):
            for k in range(lags):
                taps[c, k : k + 1, :] = mine[c : c + 1, k * GROUP : (k + 1) * GROUP]

        def place(u):
            return jnp.clip(jnp.where(u < count0, u, slots + u - count0), 0, own - 1)

        def beyond(q):
            return jnp.clip(own + q - n, 0, own + reach - 1)

        for q in range(reach):
            tab[t_s + q] = jnp.where(q < n, place(n - 1 - q), beyond(q))
            tab[t_t + q] = jnp.where(q < n, place(q), beyond(q))
        for r in range(own + reach):
            tab[t_w + r] = own + reach - 1 - r if r < reach else place(r - reach)
            tab[t_v + r] = jnp.where(r < n, place(r), beyond(r))
        for j in range(slots):
            at0 = jnp.where(j < count0, j, own)
            at1 = jnp.where(j < count1, j + count0, own)
            tab[t_mine + j] = jnp.where(side == 0, at0, at1)
            tab[t_theirs + j] = jnp.where(side == 0, at1, at0)

        def put(mask, at, ok):
            value = ok.astype(jnp.int32).astype(f32)
            mask[at] = jnp.full((16, GROUP), value, f32).astype(bf16)

        for u in range(own):
            for k in range(lags):
                live = u < n
                found = support_ref[k, jnp.clip(first + u, 0, total - 1)] >= 0
                put(fmask_ref, u * lags + lags - 1 - k, live & found)
                later = first + u + k
                found = support_ref[k, jnp.clip(later, 0, total - 1)] >= 0
                put(bmask_ref, u * lags + k, live & found & (later < total))

    for c in range(min(LEAD, chunks)):
        launch(c)
    make_tables()

    @pl.loop(0, chunks + LAG)
    def _(s):
        if LEAD < chunks:
            @pl.when(s + LEAD < chunks)
            def _():
                launch(s + LEAD)

        @pl.when(s < chunks)
        def _():
            gather_pair(s)

        @pl.when((s >= 1) & (s < chunks + 1))
        def _():
            relay(s - 1)

        @pl.when((s >= 2) & (s < chunks + 2))
        def _():
            work(s - 2)

        for b, (start, size) in enumerate(batches):
            @pl.when(s == start + size + 1)
            def _():
                sum_over_ch(b)

            @pl.when(s == start + size + 2)
            def _():
                sum_over_ctx(b)

        @pl.when(s == chunks + 3)
        def _():
            end_sums()

        @pl.when(s >= LAG)
        def _():
            finish(s - LAG)

    for b in range(2):
        @pl.loop(1, n_ch)
        def _(d):
            over_ch(b, d, my_ch).wait_send()

        @pl.loop(1, n_ctx)
        def _(d):
            over_ctx(b, d, me).wait_send()

    @pl.loop(0, chunks)
    def _(c):
        for kind in range(2):
            store(kind, side, c).wait()
            store(kind, far, c).wait()
        x_copy(c).wait_send()
        w_copy(c).wait_send()
        a_copy(c).wait_send()
        c_copy(c).wait_send()

        @pl.when(has_up)
        def _():
            x_up(c, 0).wait_send()
            x_up(c, 1).wait_send()

        @pl.when(has_down)
        def _():
            w_down(c, 0).wait_send()
            w_down(c, 1).wait_send()


def hand_over(slots, gg_in, ig_in, fg_in, gg_out, ig_out, fg_out, gg, ig, fg, sem, fg_sem):
    rows = gg_in.shape[1] // 2
    loads = [pltpu.make_async_copy(fg_in, fg, fg_sem.at[0])]
    stores = [pltpu.make_async_copy(fg, fg_out, fg_sem.at[1])]
    for j in range(slots):
        for part in range(2):
            for kind, (src, mid, dst) in enumerate(((gg_in, gg, gg_out), (ig_in, ig, ig_out))):
                at = (j, pl.ds(part * rows, rows))
                sems = sem.at[0, kind, j, part], sem.at[1, kind, j, part]
                loads.append(pltpu.make_async_copy(src.at[at], mid.at[at], sems[0]))
                stores.append(pltpu.make_async_copy(mid.at[at], dst.at[at], sems[1]))
    for load in loads:
        load.start()
    for load, store in zip(loads, stores):
        load.wait()
        store.start()
    for store in stores:
        store.wait()


def per_device(conv_input, gate_signal, cotangent, filters, tile_owner, support):
    slots, rows, channels = conv_input.shape
    lags = support.shape[1]
    filter_count, taps = filters.shape
    n_ctx = lax.axis_size("ctx")
    n_ch = lax.axis_size("ch")
    half = channels // 2
    chunks = half // GROUP
    own, reach = 2 * slots, lags - 1
    norm = 1.0 / math.sqrt(
        tile_owner.shape[0] * rows * channels * lax.axis_size("ch") / filter_count
    )
    bf16, f32 = jnp.bfloat16, jnp.float32
    vmem = pl.BlockSpec(memory_space=pltpu.VMEM)
    whole = jax.ShapeDtypeStruct(conv_input.shape, bf16)
    part = lambda count: pltpu.VMEM((chunks, count, rows, GROUP), bf16)
    hbm = pl.BlockSpec(memory_space=pl.ANY)
    results = pl.pallas_call(
        functools.partial(kernel, n_ctx, n_ch, norm),
        out_shape=(whole, whole, jax.ShapeDtypeStruct(filters.shape, f32)),
        in_specs=[pl.BlockSpec(memory_space=pltpu.SMEM)] * 2 + [hbm] * 3 + [vmem],
        out_specs=(hbm, hbm, vmem),
        scratch_shapes=[
            part(slots),
            part(slots),
            part(slots),
            part(slots),
            part(slots),
            part(slots),
            part(slots),
            part(slots),
            part(slots),
            part(slots),
            part(slots),
            part(slots),
            part(reach),
            part(reach),
            part(reach),
            part(reach),
            part(slots),
            part(slots),
            part(slots),
            part(slots),
            part(own + reach),
            part(own + reach),
            pltpu.VMEM((rows, lags * rows), bf16),
            pltpu.VMEM((rows, lags * rows), bf16),
            pltpu.VMEM((lags * rows, own * GROUP), bf16),
            pltpu.VMEM((rows, own * GROUP), bf16),
            pltpu.VMEM((own + 1, rows, GROUP), f32),
            pltpu.VMEM((own + 1, rows, GROUP), f32),
            pltpu.SMEM((52,), jnp.int32),
            pltpu.VMEM((chunks, lags, GROUP), f32),
            pltpu.VMEM((own * lags, 16, GROUP), bf16),
            pltpu.VMEM((own * lags, 16, GROUP), bf16),
            pltpu.VMEM((chunks, lags, GROUP), f32),
            pltpu.VMEM((chunks, lags, GROUP), f32),
            pltpu.VMEM((n_ch, chunks, lags, GROUP), f32),
            pltpu.VMEM((n_ctx, chunks, lags, GROUP), f32),
            pltpu.SemaphoreType.DMA((4, chunks)),
            pltpu.SemaphoreType.DMA((4, chunks)),
            pltpu.SemaphoreType.DMA((4, chunks)),
            pltpu.SemaphoreType.DMA((4, chunks)),
            pltpu.SemaphoreType.DMA((2, n_ch)),
            pltpu.SemaphoreType.DMA((2, n_ch)),
            pltpu.SemaphoreType.DMA((2, n_ctx)),
            pltpu.SemaphoreType.DMA((2, n_ctx)),
            pltpu.SemaphoreType.DMA((2, 2, chunks)),
            pltpu.SemaphoreType.DMA((2, chunks)),
            pltpu.SemaphoreType.DMA((2, 2, chunks)),
        ],
        compiler_params=pltpu.CompilerParams(
            collective_id=0, has_side_effects=True, vmem_limit_bytes=56 * 2**20
        ),
        cost_estimate=pl.CostEstimate(
            flops=6 * rows * rows * own * lags * half,
            bytes_accessed=10 * slots * rows * channels,
            transcendentals=0,
        ),
    )(tile_owner, support.T, conv_input, gate_signal, cotangent, filters)
    return pl.pallas_call(
        functools.partial(hand_over, slots),
        out_shape=(whole, whole, jax.ShapeDtypeStruct(filters.shape, f32)),
        in_specs=[hbm] * 3,
        out_specs=(hbm,) * 3,
        scratch_shapes=[
            pltpu.VMEM(conv_input.shape, bf16),
            pltpu.VMEM(conv_input.shape, bf16),
            pltpu.VMEM(filters.shape, f32),
            pltpu.SemaphoreType.DMA((2, 2, slots, 2)),
            pltpu.SemaphoreType.DMA((2,)),
        ],
        compiler_params=pltpu.CompilerParams(vmem_limit_bytes=60 * 2**20),
        cost_estimate=pl.CostEstimate(
            flops=0, bytes_accessed=8 * slots * rows * channels, transcendentals=0
        ),
    )(*results)


def solution(mesh):
    return jax.shard_map(
        per_device,
        mesh=mesh,
        in_specs=(P("ctx", None, "ch"), P("ctx", None, "ch"), P("ctx", None, "ch"), P(), P(), P()),
        out_specs=(P("ctx", None, "ch"), P("ctx", None, "ch"), P()),
        check_vma=False,
    )
```
